32 devices in a mesh: ev: 8 (over z, x), node: 4 (over y, core).
Axes of the slice: x: 2, y: 2, z: 4, core: 2. Of those that a mesh axis runs over, the one named last changes fastest.
Arguments:
- src_owner: int32 [16384, 1], P(('ev', 'node')), may hold values from 0 to 31; in each aligned block of 512 rows (0 to 511, 512 to 1023, ...) at most 32 rows name the same one
- src_row: int32 [16384], P(('ev', 'node')), may hold values from 0 to 4095
- dst_owner: int32 [16384, 1], P(('ev', 'node')), may hold values from 0 to 31; in each aligned block of 512 rows (0 to 511, 512 to 1023, ...) at most 32 rows name the same one
- dst_row: int32 [16384], P(('ev', 'node')), may hold values from 0 to 4095
- event_time: int32 [16384], P(('ev', 'node')), may hold values from 4096 to 8191
- edge_feat: bfloat16 [16384, 256], P(('ev', 'node')), may hold values from -6 to 6
- memory: bfloat16 [131072, 256], P(('ev', 'node')), may hold values from -3 to 3
- last_update: int32 [131072], P(('ev', 'node')), may hold values from 0 to 4095
- time_freq: float32 [128], replicated, may hold values from 0.0001 to 1
- time_phase: float32 [128], replicated, may hold values from -3.140625 to 3.140625
- w_msg_in: bfloat16 [896, 512], replicated, may hold values from -0.1875 to 0.1875
- b_msg: float32 [512], replicated, may hold values from -3 to 3
- w_msg_out: bfloat16 [512, 256], replicated, may hold values from -0.25 to 0.25
- w_gru_in: bfloat16 [256, 768], replicated, may hold values from -0.375 to 0.375
- b_gru_in: float32 [768], replicated, may hold values from -3 to 3
- w_gru_hid: bfloat16 [256, 768], replicated, may hold values from -0.375 to 0.375
Outputs:
- new_memory: bfloat16 [131072, 256], P(('ev', 'node'))
The draws below stay inside these ranges and needn't reach their ends.
Inputs may be any that keep to these rules, and one draw needn't show every extreme that they name: `src_owner`: within the events of one device (aligned blocks of 512 rows) no owner is named by more than 32 events, a bound that some block reaches. `dst_owner`: within the events of one device (aligned blocks of 512 rows) no owner is named by more than 32 events, a bound that some block reaches. `event_time`: every event is later than the last update of either of its nodes.
All inputs are finite; a program needn't handle non-finite values.
Results may differ from the reference program's by a relative error of at most 0.0021.
Values may be sent and summed in bfloat16 or wider, within the bound.
A program may use at most 64 MiB of HBM per device.

```python
import math
import jax
import jax.numpy as jnp
import numpy as np

M = 256
TD = 128
FE = 256
HID = 512
MSG = 256
TIME_SPAN = 4096
EV_DEV = 512
ROWS_DEV = 4096
EVENTS = 16384
NODES = 131072
CAP = 32
DEVICES = 32


def with_ends(drawn, stream_key, low, top_value):
    longest = drawn.shape.index(max(drawn.shape))
    spots = []
    for shift in (0, 1):
        where = [jax.random.randint(jax.random.fold_in(stream_key, axis), (), 0, length) for axis, length in enumerate(drawn.shape)]
        where[longest] = (where[longest] + shift) % drawn.shape[longest]
        spots.append(tuple(where))
    return drawn.at[spots[0]].set(low).at[spots[1]].set(top_value)


def block_scale(stream_key, extent, cuts, low, largest):
    level = 1.0
    for position, blocks in cuts:
        steps = jax.random.uniform(jax.random.fold_in(jax.random.fold_in(stream_key, 6), position), (blocks,), jnp.float32, low / len(cuts), largest / len(cuts))
        level = level * jnp.repeat(jnp.exp(steps), extent[position] // blocks).reshape((-1,) + (1,) * (len(extent) - 1 - position))
    return level


def shared_out(own_key, own, number, rows, amount, top, bound, skew):
    sequence = jax.random.permutation(own_key, amount)
    packed, common = shares(amount, rows * top, bound, skew, True), shares(amount, rows * top, bound, skew, False)
    places = jnp.arange(amount)

    def named(lengths, offset_by):
        used = int((lengths > 0).sum())
        fixed = max(1, used // 4)
        moved = fixed + (places - fixed + offset_by * (used - fixed)) % max(1, amount - fixed)
        return jnp.zeros((amount,), jnp.int32).at[sequence[jnp.where(places < fixed, places, moved)]].set(jnp.asarray(lengths, jnp.int32))

    lengths = jnp.where(number % 4 == 0, named(packed, number // 4), named(common, number - number // 4 - 1))
    mixed = jax.random.permutation(jax.random.fold_in(own, 3), amount)
    source_of, taker = mixed[0:amount // 2 * 2:2], mixed[1:amount // 2 * 2:2]
    margin = jnp.minimum(lengths[source_of] - 1, bound - lengths[taker]) // 2
    margin = jnp.where((source_of == sequence[0]) | (taker == sequence[0]) | (lengths[taker] == 0), 0, jnp.maximum(margin, 0))
    moved = jax.random.randint(jax.random.fold_in(own, 4), (amount // 2,), 0, 1 << 20) % (margin + 1)
    lengths = lengths.at[source_of].add(-moved).at[taker].add(moved)
    labels = jnp.searchsorted(jnp.cumsum(lengths), jnp.arange(rows * top), side="right").astype(jnp.int32)
    table = labels.reshape(top, rows).T
    table = table[jax.random.permutation(jax.random.fold_in(own, 1), rows)]
    offset_by = jax.random.randint(jax.random.fold_in(own, 2), (rows, 1), 0, top)
    return jnp.take_along_axis(table, (jnp.arange(top)[None, :] + offset_by) % top, axis=1)


def shares(count, total, reach, skew, full):
    loads = [(1 << 20) // math.isqrt(standing ** skew) + 1 for standing in range(1, count + 1)]
    largest = reach if full else min(reach, max(-(-total // count), total * loads[0] // sum(loads)))
    least = 1 if total - largest >= count - 1 else 0
    counts, spare = [largest] + [least] * (count - 1), total - largest - least * (count - 1)
    while spare > 0:
        movable = [i for i in range(1, count) if counts[i] < largest] or [i for i in range(1, count) if counts[i] < reach]
        mass, budget = sum([loads[i] for i in movable]), spare
        for i in movable:
            more = min(reach - counts[i], max(1, budget * loads[i] // mass), spare)
            counts[i] = counts[i] + more
            spare = spare - more
    return np.array(counts)


def bell_draw(stream_key, shape, scale, reach, cuts=(), held_as=jnp.bfloat16):
    values = jax.random.normal(stream_key, shape, jnp.float32) * scale
    if len(cuts) > 0:
        values = block_scale(stream_key, shape, cuts, -0.22, 0.18) * values
    return jnp.clip(values, min=-reach, max=reach).astype(held_as)


def setup_inputs(seed: int = 0) -> dict:
    seeds = jax.random.split(jax.random.key(seed), 17)
    src_owner_keys = jax.random.split(jax.random.fold_in(seeds[0], 1), EVENTS // EV_DEV)
    src_owner_turns = jax.random.permutation(jax.random.fold_in(seeds[0], 3), EVENTS // EV_DEV)
    src_owner = jax.vmap(lambda own, number: shared_out(jax.random.fold_in(seeds[0], 2), own, number, EV_DEV, DEVICES, 1, CAP, 2))(src_owner_keys, src_owner_turns).reshape((EVENTS, 1))
    src_row = with_ends(jax.random.randint(seeds[1], (EVENTS,), 0, ROWS_DEV), jax.random.fold_in(seeds[1], 1), 0, ROWS_DEV - 1).astype(jnp.int32)
    dst_owner_keys = jax.random.split(jax.random.fold_in(seeds[2], 1), EVENTS // EV_DEV)
    dst_owner_turns = jax.random.permutation(jax.random.fold_in(seeds[2], 3), EVENTS // EV_DEV)
    dst_owner = jax.vmap(lambda own, number: shared_out(jax.random.fold_in(seeds[2], 2), own, number, EV_DEV, DEVICES, 1, CAP, 2))(dst_owner_keys, dst_owner_turns).reshape((EVENTS, 1))
    dst_row = with_ends(jax.random.randint(seeds[3], (EVENTS,), 0, ROWS_DEV), jax.random.fold_in(seeds[3], 1), 0, ROWS_DEV - 1).astype(jnp.int32)
    event_time = with_ends(jax.random.randint(seeds[4], (EVENTS,), TIME_SPAN, 2 * TIME_SPAN), jax.random.fold_in(seeds[4], 1), TIME_SPAN, (2 * TIME_SPAN) - 1).astype(jnp.int32)
    edge_feat = bell_draw(seeds[5], (EVENTS, FE), 1.0, 6.0, ((0, 32),))
    memory = bell_draw(seeds[6], (NODES, M), 0.5, 3.0, ((0, 32),))
    last_update = with_ends(jax.random.randint(seeds[7], (NODES,), 0, TIME_SPAN), jax.random.fold_in(seeds[7], 1), 0, TIME_SPAN - 1).astype(jnp.int32)
    time_freq = jnp.clip(jnp.exp(jax.random.uniform(seeds[8], (TD,), jnp.float32, math.log(0.0001), math.log(1.0))), 0.0001, 1.0)
    time_phase = jnp.clip(jax.random.uniform(seeds[9], (TD,), jnp.float32, -3.140625, 3.140625), -3.140625, 3.140625)
    w_msg_in = bell_draw(seeds[10], (2 * M + TD + FE, HID), (2 * M + TD + FE) ** -0.5, 0.1875)
    b_msg = bell_draw(seeds[11], (HID,), 0.5, 3.0, (), jnp.float32)
    w_msg_out = bell_draw(seeds[12], (HID, MSG), HID ** -0.5, 0.25)
    w_gru_in = bell_draw(seeds[13], (MSG, 3 * M), MSG ** -0.5, 0.375)
    b_gru_in = bell_draw(seeds[14], (3 * M,), 0.5, 3.0, (), jnp.float32)
    w_gru_hid = bell_draw(seeds[15], (M, 3 * M), M ** -0.5, 0.375)
    return {"src_owner": src_owner, "src_row": src_row, "dst_owner": dst_owner, "dst_row": dst_row, "event_time": event_time, "edge_feat": edge_feat, "memory": memory, "last_update": last_update, "time_freq": time_freq, "time_phase": time_phase, "w_msg_in": w_msg_in, "b_msg": b_msg, "w_msg_out": w_msg_out, "w_gru_in": w_gru_in, "b_gru_in": b_gru_in, "w_gru_hid": w_gru_hid}


def encode(delta_int, time_freq, time_phase):
    delta = delta_int.astype(jnp.float32)
    return jnp.cos(delta[..., None] * time_freq + time_phase).astype(jnp.bfloat16)


def gru_update(mean_msg, state, w_gru_in, b_gru_in, w_gru_hid):
    width = state.shape[-1]
    input_part = jnp.dot(mean_msg, w_gru_in, preferred_element_type=jnp.float32) + b_gru_in
    state_part = jnp.dot(state, w_gru_hid, preferred_element_type=jnp.float32)
    reset = jax.nn.sigmoid(input_part[:, :width] + state_part[:, :width])
    update = jax.nn.sigmoid(input_part[:, width:2 * width] + state_part[:, width:2 * width])
    candid = jnp.tanh(input_part[:, 2 * width:] + reset * state_part[:, 2 * width:])
    return ((1.0 - update) * candid + update * state.astype(jnp.float32)).astype(jnp.bfloat16)


def message_net(inputs, w_msg_in, b_msg, w_msg_out):
    hidden = jax.nn.relu(jnp.dot(inputs, w_msg_in, preferred_element_type=jnp.float32) + b_msg).astype(jnp.bfloat16)
    return jnp.dot(hidden, w_msg_out, preferred_element_type=jnp.float32).astype(jnp.bfloat16)


def reference(src_owner, src_row, dst_owner, dst_row, event_time, edge_feat, memory, last_update, time_freq, time_phase, w_msg_in, b_msg, w_msg_out, w_gru_in, b_gru_in, w_gru_hid):
    src_node = (src_owner[:, 0] * ROWS_DEV + src_row).astype(jnp.int32)
    dst_node = (dst_owner[:, 0] * ROWS_DEV + dst_row).astype(jnp.int32)
    mem_src = memory[src_node]
    mem_dst = memory[dst_node]
    enc_src = encode(event_time - last_update[src_node], time_freq, time_phase)
    enc_dst = encode(event_time - last_update[dst_node], time_freq, time_phase)
    msg_src = message_net(jnp.concatenate([mem_src, mem_dst, enc_src, edge_feat], axis=1), w_msg_in, b_msg, w_msg_out)
    msg_dst = message_net(jnp.concatenate([mem_dst, mem_src, enc_dst, edge_feat], axis=1), w_msg_in, b_msg, w_msg_out)
    targets = jnp.concatenate([src_node, dst_node])
    messages = jnp.concatenate([msg_src, msg_dst], axis=0)
    total = jnp.zeros((NODES, messages.shape[1]), jnp.float32).at[targets].add(messages.astype(jnp.float32))
    count = jnp.zeros((NODES,), jnp.int32).at[targets].add(1)
    divisor = jnp.maximum(count[targets], 1).astype(jnp.float32)
    mean_msg = (total[targets] / divisor[:, None]).astype(jnp.bfloat16)
    new_state = gru_update(mean_msg, memory[targets], w_gru_in, b_gru_in, w_gru_hid)
    return memory.at[targets].set(new_state)
```

```python
import functools

import jax
import jax.numpy as jnp
from jax import lax
from jax.experimental import pallas as pl
from jax.experimental.pallas import tpu as pltpu
from jax.sharding import PartitionSpec as P

MESH = pl.DeviceIdType.MESH
LANES = 128
F32 = jnp.float32
BF16 = jnp.bfloat16


def mm(a, b):
    return jnp.dot(a, b, preferred_element_type=F32)


def lanes_of(shape):
    return lax.broadcasted_iota(jnp.int32, shape, 1)


def subs_of(shape):
    return lax.broadcasted_iota(jnp.int32, shape, 0)


def exchange_kernel(
    n,
    per_row,
    slots,
    ints_ref,
    edge_ref,
    mem_ref,
    last_ref,
    freq_ref,
    phase_ref,
    win_ref,
    bmsg_ref,
    wout_ref,
    arrived_ref,
    rflat_ref,
    req_send,
    req_recv,
    rows_col,
    last_send,
    last_recv,
    row_send,
    row_recv,
    msg_send,
    msg_recv,
    msgs,
    send_sems,
    recv_sems,
):
    ev = lax.axis_index("ev")
    me = ev * per_row + lax.axis_index("node")
    events = edge_ref.shape[0]
    rows_count, width = mem_ref.shape
    hidden = wout_ref.shape[0]
    time_width = freq_ref.shape[1]
    cap = slots // 2
    rep = LANES // slots
    total = n * slots
    group = 256 // slots
    groups = n // group

    def coords(device):
        return (device // per_row, device % per_row)

    barrier = pltpu.get_barrier_semaphore()

    @pl.loop(1, n)
    def _(step):
        pl.semaphore_signal(
            barrier, inc=1, device_id=coords((me + step) % n), device_id_type=MESH
        )

    ints = ints_ref[...]
    padded = jnp.concatenate(
        [ints.astype(F32), jnp.zeros((LANES - 8, events), F32)], axis=0
    )
    cols = padded.T
    lane_e = lanes_of((events, LANES))
    sub_e = subs_of((LANES, events))
    tri_low = (lanes_of((events, events)) < subs_of((events, events))).astype(F32).astype(BF16)
    tri_up = (subs_of((events, events)) < lanes_of((events, events))).astype(F32).astype(BF16)

    hit_col, pos_col, slot_col, slot_row = [], [], [], []
    req_hi = jnp.zeros((LANES, LANES), F32)
    req_lo = jnp.zeros((LANES, LANES), F32)
    for side in range(2):
        owner_c = cols[:, side : side + 1].astype(jnp.int32)
        row_c = cols[:, 2 + side : 3 + side].astype(jnp.int32)
        hit_c = (owner_c == lane_e).astype(F32)
        hit_cb = hit_c.astype(BF16)
        pos_c = jnp.sum(mm(tri_low, hit_cb) * hit_c, axis=1, keepdims=True).astype(jnp.int32)
        pos_c = pos_c + side * cap
        owner_r = ints[side : side + 1, :]
        hit_r = (owner_r == sub_e).astype(F32)
        hit_rb = hit_r.astype(BF16)
        pos_r = jnp.sum(mm(hit_rb, tri_up) * hit_r, axis=0, keepdims=True).astype(jnp.int32)
        pos_r = pos_r + side * cap
        place = pos_c == lane_e % slots
        req_hi += mm(hit_rb, jnp.where(place, (row_c // 64 + 1).astype(F32), 0.0).astype(BF16))
        req_lo += mm(hit_rb, jnp.where(place, (row_c % 64).astype(F32), 0.0).astype(BF16))
        hit_col.append(hit_cb)
        pos_col.append(pos_c)
        slot_col.append(owner_c * slots + pos_c)
        slot_row.append(owner_r * slots + pos_r)
    request = jnp.where(req_hi > 0.5, (req_hi - 1.0) * 64.0 + req_lo, -1.0).astype(jnp.int32)
    for j in range(n):
        req_send[j] = request[j : j + 1, :]

    pl.semaphore_wait(barrier, n - 1)

    def send(phase, src, dst, device):
        return pltpu.make_async_remote_copy(
            src_ref=src,
            dst_ref=dst,
            send_sem=send_sems.at[phase],
            recv_sem=recv_sems.at[phase],
            device_id=coords(device),
            device_id_type=MESH,
        )

    def drain(sem, buf):
        part = buf.at[pl.ds(0, n - 1)]
        pltpu.make_async_copy(part, part, sem).wait()

    @pl.loop(1, n)
    def _(step):
        peer = (me + step) % n
        send(0, req_send.at[peer], req_recv.at[me], peer).start()

    req_recv[pl.ds(me, 1)] = req_send[pl.ds(me, 1)]
    drain(recv_sems.at[0], req_recv)

    lane_1 = lanes_of((1, LANES))
    blocks = []
    for b in range(n // rep):
        block = req_recv[b * rep]
        for q in range(1, rep):
            block = jnp.where(lane_1 // slots == q, req_recv[b * rep + q], block)
        blocks.append(block)
    flat = jnp.concatenate(blocks, axis=1)
    rflat_ref[...] = flat
    square = jnp.concatenate(
        [req_recv[j].astype(F32) for j in range(n)]
        + ([jnp.zeros((LANES - n, LANES), F32)] if n < LANES else []),
        axis=0,
    ).T.astype(jnp.int32)
    for j in range(n):
        rows_col[j * slots : (j + 1) * slots, :] = square[:slots, j : j + 1]

    @pl.loop(0, groups)
    def _(step):
        g = (ev * per_row // group + 1 + step) % groups
        wanted = rows_col[pl.ds(pl.multiple_of(g * 256, 256), 256), :]
        acc = jnp.zeros((256, width), F32)
        depth = 1024
        for k in range(rows_count // depth):
            onehot = (wanted == lanes_of((256, depth)) + k * depth).astype(F32).astype(BF16)
            acc += mm(onehot, mem_ref[k * depth : (k + 1) * depth, :])
        row_send[pl.ds(g * group, group)] = acc.astype(BF16).reshape(group, slots, width)
        for t in range(group):
            peer = g * group + t

            @pl.when(peer != me)
            def _():
                send(1, row_send.at[peer], row_recv.at[me], peer).start()

    last = last_ref[...]
    high_count = rows_count // LANES
    last_hi = (last // 64).astype(F32)
    last_lo = (last % 64).astype(F32)
    fill = jnp.zeros((LANES - high_count, LANES), F32)
    table_hi = jnp.concatenate([last_hi, fill], axis=0).T.astype(BF16)
    table_lo = jnp.concatenate([last_lo, fill], axis=0).T.astype(BF16)
    onehot_hi = (flat // LANES == subs_of((LANES, total))).astype(F32).astype(BF16)
    found = mm(table_hi, onehot_hi) * 64.0 + mm(table_lo, onehot_hi)
    kept = jnp.where(flat % LANES == subs_of((LANES, total)), found, 0.0)
    picked_last = jnp.sum(kept, axis=0, keepdims=True).astype(jnp.int32)
    for b in range(n // rep):
        last_send[b] = picked_last[:, b * LANES : (b + 1) * LANES]

    @pl.loop(1, n)
    def _(step):
        peer = (me + step) % n
        send(2, last_send.at[peer // rep], last_recv.at[me], peer).start()

    last_recv[pl.ds(me, 1)] = last_send[pl.ds(me // rep, 1)]
    row_recv[pl.ds(me, 1)] = row_send[pl.ds(me, 1)]

    edge_part = mm(edge_ref[...], win_ref[2 * width + time_width :, :]) + bmsg_ref[...]

    drain(recv_sems.at[2], last_recv)
    got = jnp.concatenate(
        [last_recv[j] for j in range(n)]
        + ([jnp.zeros((LANES - n, LANES), jnp.int32)] if n < LANES else []),
        axis=0,
    )
    got_hi = (got // 64).astype(F32).astype(BF16)
    got_lo = (got % 64).astype(F32).astype(BF16)
    moment = cols[:, 4:5]
    coded = []
    for side in range(2):
        spread = mm(hit_col[side], got_hi) * 64.0 + mm(hit_col[side], got_lo)
        here = pos_col[side] + (me % rep) * slots == lane_e
        before = jnp.sum(jnp.where(here, spread, 0.0), axis=1, keepdims=True)
        angle = (moment - before) * freq_ref[...] + phase_ref[...]
        coded.append(jnp.cos(angle).astype(BF16))

    drain(recv_sems.at[1], row_recv)
    fetched = row_recv[...].reshape(total, width)
    picked = []
    for side in range(2):
        pick = (slot_col[side] == lanes_of((events, total))).astype(F32).astype(BF16)
        picked.append(mm(pick, fetched).astype(BF16))
    for side in range(2):
        inputs = jnp.concatenate([picked[side], picked[1 - side], coded[side]], axis=1)
        hid = mm(inputs, win_ref[: 2 * width + time_width, :]) + edge_part
        hid = jnp.maximum(hid, 0.0).astype(BF16)
        msgs[side * events : (side + 1) * events, :] = mm(hid, wout_ref[...]).astype(BF16)

    slot_both = jnp.concatenate(slot_row, axis=1)

    @pl.loop(0, groups)
    def _(step):
        g = (ev * per_row // group + 1 + step) % groups
        placed = slot_both == subs_of((256, 2 * events)) + g * 256
        block = mm(placed.astype(F32).astype(BF16), msgs[...])
        msg_send[pl.ds(g * group, group)] = block.astype(BF16).reshape(group, slots, block.shape[1])
        for t in range(group):
            peer = g * group + t

            @pl.when(peer != me)
            def _():
                send(3, msg_send.at[peer], msg_recv.at[me], peer).start()

    msg_recv[pl.ds(me, 1)] = msg_send[pl.ds(me, 1)]
    drain(send_sems.at[0], req_send)
    drain(send_sems.at[1], row_send)
    drain(send_sems.at[2], last_recv)
    drain(recv_sems.at[3], msg_recv)
    arrived_ref[...] = msg_recv[...].reshape(arrived_ref.shape)
    drain(send_sems.at[3], msg_send)


def update_kernel(rflat_ref, msg_ref, mem_ref, win_ref, bin_ref, whid_ref, out_ref):
    rows, width = mem_ref.shape
    total = msg_ref.shape[0]
    base = pl.program_id(0) * rows
    hits = (rflat_ref[...] == subs_of((rows, total)) + base).astype(F32)
    count = jnp.sum(hits, axis=1, keepdims=True)
    summed = mm(hits.astype(BF16), msg_ref[...])
    mean = (summed / jnp.maximum(count, 1.0)).astype(BF16)
    state = mem_ref[...]
    gi = mm(mean, win_ref[...]) + bin_ref[...]
    gh = mm(state, whid_ref[...])
    reset = jax.nn.sigmoid(gi[:, :width] + gh[:, :width])
    update = jax.nn.sigmoid(gi[:, width : 2 * width] + gh[:, width : 2 * width])
    candid = jnp.tanh(gi[:, 2 * width :] + reset * gh[:, 2 * width :])
    fresh = (1.0 - update) * candid + update * state.astype(F32)
    out_ref[...] = jnp.where(count > 0.5, fresh, state.astype(F32)).astype(BF16)


def local(
    per_row,
    src_owner,
    src_row,
    dst_owner,
    dst_row,
    event_time,
    edge_feat,
    memory,
    last_update,
    time_freq,
    time_phase,
    w_msg_in,
    b_msg,
    w_msg_out,
    w_gru_in,
    b_gru_in,
    w_gru_hid,
):
    n = lax.axis_size(("ev", "node"))
    events = edge_feat.shape[0]
    slots = 2 * max(2, 2 * events // n)
    rows_count, width = memory.shape
    msg_width = w_msg_out.shape[1]
    total = n * slots
    zero = jnp.zeros_like(src_row)
    ints = jnp.stack(
        [src_owner[:, 0], dst_owner[:, 0], src_row, dst_row, event_time, zero, zero, zero]
    )
    vmem = pl.BlockSpec(memory_space=pltpu.VMEM)
    arrived, rflat = pl.pallas_call(
        functools.partial(exchange_kernel, n, per_row, slots),
        out_shape=(
            jax.ShapeDtypeStruct((total, msg_width), BF16),
            jax.ShapeDtypeStruct((1, total), jnp.int32),
        ),
        in_specs=[vmem] * 9,
        out_specs=(vmem, vmem),
        scratch_shapes=[
            pltpu.VMEM((n, 1, LANES), jnp.int32),
            pltpu.VMEM((n, 1, LANES), jnp.int32),
            pltpu.VMEM((total, 1), jnp.int32),
            pltpu.VMEM((n * slots // LANES, 1, LANES), jnp.int32),
            pltpu.VMEM((n, 1, LANES), jnp.int32),
            pltpu.VMEM((n, slots, width), BF16),
            pltpu.VMEM((n, slots, width), BF16),
            pltpu.VMEM((n, slots, msg_width), BF16),
            pltpu.VMEM((n, slots, msg_width), BF16),
            pltpu.VMEM((2 * events, msg_width), BF16),
            pltpu.SemaphoreType.DMA((4,)),
            pltpu.SemaphoreType.DMA((4,)),
        ],
        compiler_params=pltpu.CompilerParams(
            collective_id=0, has_side_effects=True, vmem_limit_bytes=48 * 1024 * 1024
        ),
        name="exchange",
    )(
        ints,
        edge_feat,
        memory,
        last_update.reshape(rows_count // LANES, LANES),
        time_freq[None, :],
        time_phase[None, :],
        w_msg_in,
        b_msg[None, :],
        w_msg_out,
    )
    chunk = min(512, rows_count)

    def fixed(*shape):
        return pl.BlockSpec(shape, lambda i: (0, 0))

    return pl.pallas_call(
        update_kernel,
        grid=(rows_count // chunk,),
        out_shape=jax.ShapeDtypeStruct(memory.shape, BF16),
        in_specs=[
            fixed(1, total),
            fixed(total, msg_width),
            pl.BlockSpec((chunk, width), lambda i: (i, 0)),
            fixed(*w_gru_in.shape),
            fixed(1, b_gru_in.shape[0]),
            fixed(*w_gru_hid.shape),
        ],
        out_specs=pl.BlockSpec((chunk, width), lambda i: (i, 0)),
        compiler_params=pltpu.CompilerParams(vmem_limit_bytes=48 * 1024 * 1024),
        name="update",
    )(rflat, arrived, memory, w_gru_in, b_gru_in[None, :], w_gru_hid)


def solution(mesh):
    in_specs = (
        P(("ev", "node"), None),
        P(("ev", "node")),
        P(("ev", "node"), None),
        P(("ev", "node")),
        P(("ev", "node")),
        P(("ev", "node"), None),
        P(("ev", "node"), None),
        P(("ev", "node")),
        P(),
        P(),
        P(),
        P(),
        P(),
        P(),
        P(),
        P(),
    )
    out_specs = P(("ev", "node"), None)
    return jax.shard_map(
        functools.partial(local, mesh.shape["node"]),
        mesh=mesh,
        in_specs=in_specs,
        out_specs=out_specs,
        check_vma=False,
    )
```

```python
import functools

import jax
import jax.numpy as jnp
from jax import lax
from jax.experimental import pallas as pl
from jax.experimental.pallas import tpu as pltpu
from jax.sharding import PartitionSpec as P

MESH = pl.DeviceIdType.MESH
LANES = 128
F32 = jnp.float32
BF16 = jnp.bfloat16


def mm(a, b):
    return jnp.dot(a, b, preferred_element_type=F32)


def lanes_of(shape):
    return lax.broadcasted_iota(jnp.int32, shape, 1)


def subs_of(shape):
    return lax.broadcasted_iota(jnp.int32, shape, 0)


def exchange_kernel(
    n,
    per_row,
    slots,
    events,
    time_width,
    params_hbm,
    last_hbm,
    mem_hbm,
    edge_hbm,
    win_hbm,
    wout_hbm,
    gin_hbm,
    ghid_hbm,
    out_hbm,
    params_ref,
    last_ref,
    mem_ref,
    edge_ref,
    win_ref,
    wout_ref,
    gin_ref,
    ghid_ref,
    out_ref,
    req_send,
    req_recv,
    rows_col,
    last_send,
    last_recv,
    row_send,
    row_recv,
    msg_send,
    msg_recv,
    msgs,
    flat_ref,
    hits_ref,
    count_ref,
    state_ref,
    sum_ref,
    send_sems,
    recv_sems,
    load_sems,
    store_sem,
):
    ev = lax.axis_index("ev")
    me = ev * per_row + lax.axis_index("node")
    rows_count, width = mem_ref.shape
    hidden = wout_ref.shape[0]
    cap = slots // 2
    rep = LANES // slots
    total = n * slots
    group = 256 // slots
    groups = n // group

    def coords(device):
        return (device // per_row, device % per_row)

    barrier = pltpu.get_barrier_semaphore()

    @pl.loop(1, n)
    def _(step):
        pl.semaphore_signal(
            barrier, inc=1, device_id=coords((me + step) % n), device_id_type=MESH
        )

    loads = [
        pltpu.make_async_copy(src, dst, load_sems.at[k])
        for k, (src, dst) in enumerate(
            [
                (params_hbm, params_ref),
                (last_hbm, last_ref),
                (mem_hbm, mem_ref),
                (edge_hbm, edge_ref),
                (win_hbm, win_ref),
                (wout_hbm, wout_ref),
                (ghid_hbm, ghid_ref),
                (gin_hbm, gin_ref),
            ]
        )
    ]
    for load in loads:
        load.start()
    loads[0].wait()
    params = params_ref[...]
    ints = params[:, :events].astype(jnp.int32)
    padded = jnp.concatenate(
        [params[:, :events], jnp.zeros((LANES - 8, events), F32)], axis=0
    )
    freq = params[7:8, :time_width]
    phase = params[7:8, time_width : 2 * time_width]
    gate = params[6:7, : 3 * width]
    cols = padded.T
    lane_e = lanes_of((events, LANES))
    sub_e = subs_of((LANES, events))
    tri_low = (lanes_of((events, events)) < subs_of((events, events))).astype(F32).astype(BF16)
    tri_up = (subs_of((events, events)) < lanes_of((events, events))).astype(F32).astype(BF16)

    hit_col, pos_col, slot_col, slot_row = [], [], [], []
    req_hi = jnp.zeros((LANES, LANES), F32)
    req_lo = jnp.zeros((LANES, LANES), F32)
    for side in range(2):
        owner_c = cols[:, side : side + 1].astype(jnp.int32)
        row_c = cols[:, 2 + side : 3 + side].astype(jnp.int32)
        hit_c = (owner_c == lane_e).astype(F32)
        hit_cb = hit_c.astype(BF16)
        pos_c = jnp.sum(mm(tri_low, hit_cb) * hit_c, axis=1, keepdims=True).astype(jnp.int32)
        pos_c = pos_c + side * cap
        owner_r = ints[side : side + 1, :]
        hit_r = (owner_r == sub_e).astype(F32)
        hit_rb = hit_r.astype(BF16)
        pos_r = jnp.sum(mm(hit_rb, tri_up) * hit_r, axis=0, keepdims=True).astype(jnp.int32)
        pos_r = pos_r + side * cap
        place = pos_c == lane_e % slots
        req_hi += mm(hit_rb, jnp.where(place, (row_c // 64 + 1).astype(F32), 0.0).astype(BF16))
        req_lo += mm(hit_rb, jnp.where(place, (row_c % 64).astype(F32), 0.0).astype(BF16))
        hit_col.append(hit_cb)
        pos_col.append(pos_c)
        slot_col.append(owner_c * slots + pos_c)
        slot_row.append(owner_r * slots + pos_r)
    request = jnp.where(req_hi > 0.5, (req_hi - 1.0) * 64.0 + req_lo, -1.0).astype(jnp.int32)
    for j in range(n):
        req_send[j] = request[j : j + 1, :]

    pl.semaphore_wait(barrier, n - 1)

    def send(phase, src, dst, device):
        return pltpu.make_async_remote_copy(
            src_ref=src,
            dst_ref=dst,
            send_sem=send_sems.at[phase],
            recv_sem=recv_sems.at[phase],
            device_id=coords(device),
            device_id_type=MESH,
        )

    def drain(sem, buf):
        part = buf.at[pl.ds(0, n - 1)]
        pltpu.make_async_copy(part, part, sem).wait()

    @pl.loop(1, n)
    def _(step):
        peer = (me + step) % n
        send(0, req_send.at[peer], req_recv.at[me], peer).start()

    req_recv[pl.ds(me, 1)] = req_send[pl.ds(me, 1)]
    drain(recv_sems.at[0], req_recv)

    lane_1 = lanes_of((1, LANES))
    blocks = []
    for b in range(n // rep):
        block = req_recv[b * rep]
        for q in range(1, rep):
            block = jnp.where(lane_1 // slots == q, req_recv[b * rep + q], block)
        blocks.append(block)
    flat = jnp.concatenate(blocks, axis=1)
    for g in range(groups):
        flat_ref[g] = flat[:, g * 256 : (g + 1) * 256]
    square = jnp.concatenate(
        [req_recv[j].astype(F32) for j in range(n)]
        + ([jnp.zeros((LANES - n, LANES), F32)] if n < LANES else []),
        axis=0,
    ).T.astype(jnp.int32)
    for j in range(n):
        rows_col[j * slots : (j + 1) * slots, :] = square[:slots, j : j + 1]

    loads[2].wait()

    @pl.loop(0, groups)
    def _(step):
        g = (me // group + 1 + step) % groups
        wanted = rows_col[pl.ds(pl.multiple_of(g * 256, 256), 256), :]
        acc = jnp.zeros((256, width), F32)
        depth = 1024
        for k in range(rows_count // depth):
            onehot = (wanted == lanes_of((256, depth)) + k * depth).astype(F32).astype(BF16)
            acc += mm(onehot, mem_ref[k * depth : (k + 1) * depth, :])
        row_send[pl.ds(g * group, group)] = acc.astype(BF16).reshape(group, slots, width)
        for t in range(group):
            peer = g * group + (me + t) % group

            @pl.when(peer != me)
            def _():
                send(1, row_send.at[peer], row_recv.at[me], peer).start()

    loads[1].wait()
    last = last_ref[...]
    high_count = rows_count // LANES
    last_hi = (last // 64).astype(F32)
    last_lo = (last % 64).astype(F32)
    fill = jnp.zeros((LANES - high_count, LANES), F32)
    table_hi = jnp.concatenate([last_hi, fill], axis=0).T.astype(BF16)
    table_lo = jnp.concatenate([last_lo, fill], axis=0).T.astype(BF16)
    onehot_hi = (flat // LANES == subs_of((LANES, total))).astype(F32).astype(BF16)
    found = mm(table_hi, onehot_hi) * 64.0 + mm(table_lo, onehot_hi)
    kept = jnp.where(flat % LANES == subs_of((LANES, total)), found, 0.0)
    picked_last = jnp.sum(kept, axis=0, keepdims=True).astype(jnp.int32)
    for b in range(n // rep):
        last_send[b] = picked_last[:, b * LANES : (b + 1) * LANES]

    @pl.loop(1, n)
    def _(step):
        peer = (me + step) % n
        send(2, last_send.at[peer // rep], last_recv.at[me], peer).start()

    last_recv[pl.ds(me, 1)] = last_send[pl.ds(me // rep, 1)]
    row_recv[pl.ds(me, 1)] = row_send[pl.ds(me, 1)]

    for load in loads[3:]:
        load.wait()
    edge_part = mm(edge_ref[...], win_ref[2 * width + time_width :, :]) + params[5:6, :hidden]
    chunk = 512

    @pl.loop(0, rows_count // chunk)
    def _(step):
        base = pl.multiple_of(step * chunk, chunk)
        count = jnp.zeros((chunk, 1), F32)
        for g in range(groups):
            hits = (flat_ref[g] == subs_of((chunk, 256)) + base).astype(F32)
            hits_ref[g, pl.ds(base, chunk), :] = hits.astype(BF16)
            count += jnp.sum(hits, axis=1, keepdims=True)
        count_ref[pl.ds(base, chunk), :] = count
        state_ref[pl.ds(base, chunk), :] = mm(mem_ref[pl.ds(base, chunk), :], ghid_ref[...])


    drain(recv_sems.at[2], last_recv)
    got = jnp.concatenate(
        [last_recv[j] for j in range(n)]
        + ([jnp.zeros((LANES - n, LANES), jnp.int32)] if n < LANES else []),
        axis=0,
    )
    got_hi = (got // 64).astype(F32).astype(BF16)
    got_lo = (got % 64).astype(F32).astype(BF16)
    moment = cols[:, 4:5]
    coded = []
    for side in range(2):
        spread = mm(hit_col[side], got_hi) * 64.0 + mm(hit_col[side], got_lo)
        here = pos_col[side] + (me % rep) * slots == lane_e
        before = jnp.sum(jnp.where(here, spread, 0.0), axis=1, keepdims=True)
        angle = (moment - before) * freq + phase
        coded.append(jnp.cos(angle).astype(BF16))

    drain(recv_sems.at[1], row_recv)
    fetched = row_recv[...].reshape(total, width)
    picked = []
    for side in range(2):
        pick = (slot_col[side] == lanes_of((events, total))).astype(F32).astype(BF16)
        picked.append(mm(pick, fetched).astype(BF16))
    for side in range(2):
        inputs = jnp.concatenate([picked[side], picked[1 - side], coded[side]], axis=1)
        hid = mm(inputs, win_ref[: 2 * width + time_width, :]) + edge_part
        hid = jnp.maximum(hid, 0.0).astype(BF16)
        msgs[side * events : (side + 1) * events, :] = mm(hid, wout_ref[...]).astype(BF16)

    slot_both = jnp.concatenate(slot_row, axis=1)

    half = groups // 2

    def push(first, stop, kind):
        @pl.loop(first, stop)
        def _(step):
            g = (me // group + 1 + step) % groups
            placed = slot_both == subs_of((256, 2 * events)) + g * 256
            block = mm(placed.astype(F32).astype(BF16), msgs[...])
            msg_send[pl.ds(g * group, group)] = block.astype(BF16).reshape(
                group, slots, block.shape[1]
            )
            for t in range(group):
                peer = g * group + (me + t) % group

                @pl.when(peer != me)
                def _():
                    send(kind, msg_send.at[peer], msg_recv.at[me], peer).start()

    push(0, half, 3)
    push(half, groups, 4)
    msg_recv[pl.ds(me, 1)] = msg_send[pl.ds(me, 1)]
    drain(send_sems.at[0], req_send)
    drain(send_sems.at[1], row_send)
    drain(send_sems.at[2], last_recv)

    def settle(sem, buf, blocks_moved):
        part = buf.at[pl.ds(0, blocks_moved)]
        pltpu.make_async_copy(part, part, sem).wait()

    def gathered(base, steps):
        acc = jnp.zeros((chunk, msgs.shape[1]), F32)
        for step in steps:
            g = (me // group + groups - 1 - step) % groups
            block = msg_recv[pl.ds(g * group, group)].reshape(256, msgs.shape[1])
            acc += mm(hits_ref[g, pl.ds(base, chunk), :], block)
        return acc

    settle(recv_sems.at[3], msg_recv, half * group)

    @pl.loop(0, rows_count // chunk)
    def _(step):
        base = pl.multiple_of(step * chunk, chunk)
        sum_ref[pl.ds(base, chunk), :] = gathered(base, range(half))

    settle(recv_sems.at[4], msg_recv, half * group - 1)

    @pl.loop(0, rows_count // chunk)
    def _(step):
        base = pl.multiple_of(step * chunk, chunk)
        rows = pl.ds(base, chunk)
        count = count_ref[rows, :]
        summed = sum_ref[rows, :] + gathered(base, range(half, groups))
        mean = (summed / jnp.maximum(count, 1.0)).astype(BF16)
        state = mem_ref[rows, :].astype(F32)
        gi = mm(mean, gin_ref[...]) + gate
        gh = state_ref[rows, :]
        reset = 0.5 * jnp.tanh(0.5 * (gi[:, :width] + gh[:, :width])) + 0.5
        update = 0.5 * jnp.tanh(0.5 * (gi[:, width : 2 * width] + gh[:, width : 2 * width])) + 0.5
        candid = jnp.tanh(gi[:, 2 * width :] + reset * gh[:, 2 * width :])
        fresh = candid + update * (state - candid)
        out_ref[rows, :] = jnp.where(count > 0.5, fresh, state).astype(BF16)
        pltpu.make_async_copy(out_ref.at[rows], out_hbm.at[rows], store_sem).start()

    settle(send_sems.at[3], msg_send, half * group)
    settle(send_sems.at[4], msg_send, half * group - 1)
    pltpu.make_async_copy(out_ref, out_hbm, store_sem).wait()


def local(
    per_row,
    src_owner,
    src_row,
    dst_owner,
    dst_row,
    event_time,
    edge_feat,
    memory,
    last_update,
    time_freq,
    time_phase,
    w_msg_in,
    b_msg,
    w_msg_out,
    w_gru_in,
    b_gru_in,
    w_gru_hid,
):
    n = lax.axis_size(("ev", "node"))
    events = edge_feat.shape[0]
    slots = 2 * max(2, 2 * events // n)
    rows_count, width = memory.shape
    msg_width = w_msg_out.shape[1]
    total = n * slots
    span = max(events, 3 * width, w_msg_out.shape[0], 2 * time_freq.shape[0])
    small = [
        src_owner[:, 0],
        dst_owner[:, 0],
        src_row,
        dst_row,
        event_time,
        b_msg,
        b_gru_in,
        jnp.concatenate([time_freq, time_phase]),
    ]
    params = jnp.stack([jnp.pad(x.astype(F32), (0, span - x.shape[0])) for x in small])
    operands = (
        params,
        last_update.reshape(rows_count // LANES, LANES),
        memory,
        edge_feat,
        w_msg_in,
        w_msg_out,
        w_gru_in,
        w_gru_hid,
    )
    anywhere = pl.BlockSpec(memory_space=pl.ANY)
    return pl.pallas_call(
        functools.partial(exchange_kernel, n, per_row, slots, events, time_freq.shape[0]),
        out_shape=jax.ShapeDtypeStruct(memory.shape, BF16),
        in_specs=[anywhere] * len(operands),
        out_specs=anywhere,
        scratch_shapes=[pltpu.VMEM(x.shape, x.dtype) for x in operands]
        + [
            pltpu.VMEM(memory.shape, BF16),
            pltpu.VMEM((n, 1, LANES), jnp.int32),
            pltpu.VMEM((n, 1, LANES), jnp.int32),
            pltpu.VMEM((total, 1), jnp.int32),
            pltpu.VMEM((n * slots // LANES, 1, LANES), jnp.int32),
            pltpu.VMEM((n, 1, LANES), jnp.int32),
            pltpu.VMEM((n, slots, width), BF16),
            pltpu.VMEM((n, slots, width), BF16),
            pltpu.VMEM((n, slots, msg_width), BF16),
            pltpu.VMEM((n, slots, msg_width), BF16),
            pltpu.VMEM((2 * events, msg_width), BF16),
            pltpu.VMEM((total // 256, 1, 256), jnp.int32),
            pltpu.VMEM((total // 256, rows_count, 256), BF16),
            pltpu.VMEM((rows_count, 1), F32),
            pltpu.VMEM((rows_count, 3 * width), F32),
            pltpu.VMEM((rows_count, msg_width), F32),
            pltpu.SemaphoreType.DMA((5,)),
            pltpu.SemaphoreType.DMA((5,)),
            pltpu.SemaphoreType.DMA((len(operands),)),
            pltpu.SemaphoreType.DMA,
        ],
        compiler_params=pltpu.CompilerParams(
            collective_id=0, has_side_effects=True, vmem_limit_bytes=58 * 1024 * 1024
        ),
        name="exchange",
    )(*operands)


def solution(mesh):
    in_specs = (
        P(("ev", "node"), None),
        P(("ev", "node")),
        P(("ev", "node"), None),
        P(("ev", "node")),
        P(("ev", "node")),
        P(("ev", "node"), None),
        P(("ev", "node"), None),
        P(("ev", "node")),
        P(),
        P(),
        P(),
        P(),
        P(),
        P(),
        P(),
        P(),
    )
    out_specs = P(("ev", "node"), None)
    return jax.shard_map(
        functools.partial(local, mesh.shape["node"]),
        mesh=mesh,
        in_specs=in_specs,
        out_specs=out_specs,
        check_vma=False,
    )
```

```python
import functools

import jax
import jax.numpy as jnp
from jax import lax
from jax.experimental import pallas as pl
from jax.experimental.pallas import tpu as pltpu
from jax.sharding import PartitionSpec as P

MESH = pl.DeviceIdType.MESH
LANES = 128
F32 = jnp.float32
BF16 = jnp.bfloat16


def mm(a, b):
    return jnp.dot(a, b, preferred_element_type=F32)


def lanes_of(shape):
    return lax.broadcasted_iota(jnp.int32, shape, 1)


def subs_of(shape):
    return lax.broadcasted_iota(jnp.int32, shape, 0)


def exchange_kernel(
    n,
    per_row,
    slots,
    events,
    time_width,
    so_hbm,
    do_hbm,
    sr_hbm,
    dr_hbm,
    et_hbm,
    freq_hbm,
    phase_hbm,
    bmsg_hbm,
    bgru_hbm,
    last_hbm,
    mem_hbm,
    edge_hbm,
    win_hbm,
    wout_hbm,
    gin_hbm,
    ghid_hbm,
    out_hbm,
    so_ref,
    do_ref,
    sr_ref,
    dr_ref,
    et_ref,
    freq_ref,
    phase_ref,
    bmsg_ref,
    bgru_ref,
    last_ref,
    mem_ref,
    edge_ref,
    win_ref,
    wout_ref,
    gin_ref,
    ghid_ref,
    out_ref,
    req_send,
    req_recv,
    rows_col,
    pick_ref,
    place_ref,
    last_send,
    last_recv,
    row_send,
    row_recv,
    msg_send,
    msg_recv,
    msgs,
    flat_ref,
    hits_ref,
    count_ref,
    state_ref,
    sum_ref,
    send_sems,
    recv_sems,
    load_sems,
    store_sem,
):
    ev = lax.axis_index("ev")
    me = ev * per_row + lax.axis_index("node")
    rows_count, width = mem_ref.shape
    hidden = wout_ref.shape[0]
    cap = slots // 2
    rep = LANES // slots
    total = n * slots
    group = 256 // slots
    groups = n // group

    def coords(device):
        return (device // per_row, device % per_row)

    def mirrored(step):
        k = (step + groups // 2) % groups
        k = k + (step // (groups // 2)) * (groups // 2 - 1 - 2 * k)
        g, unit = 0, 1
        while unit < groups:
            g = g + unit * ((me // group // unit + k // unit) % 2)
            unit = 2 * unit
        return g

    barrier = pltpu.get_barrier_semaphore()

    @pl.loop(1, n)
    def _(step):
        pl.semaphore_signal(
            barrier, inc=1, device_id=coords((me + step) % n), device_id_type=MESH
        )

    loads = [
        pltpu.make_async_copy(src, dst, load_sems.at[k])
        for k, (src, dst) in enumerate(
            [
                (so_hbm, so_ref),
                (do_hbm, do_ref),
                (sr_hbm, sr_ref),
                (dr_hbm, dr_ref),
                (et_hbm, et_ref),
                (last_hbm, last_ref),
                (freq_hbm, freq_ref),
                (phase_hbm, phase_ref),
                (bmsg_hbm, bmsg_ref),
                (bgru_hbm, bgru_ref),
                (mem_hbm, mem_ref),
                (edge_hbm, edge_ref),
                (win_hbm, win_ref),
                (wout_hbm, wout_ref),
                (ghid_hbm, ghid_ref),
                (gin_hbm, gin_ref),
            ]
        )
    ]
    for load in loads:
        load.start()
    for load in loads[:5]:
        load.wait()
    ints = jnp.concatenate(
        [so_ref[...], do_ref[...], sr_ref[...], dr_ref[...], et_ref[...]]
        + [jnp.zeros((3, events), jnp.int32)],
        axis=0,
    )
    padded = jnp.concatenate(
        [ints.astype(F32), jnp.zeros((LANES - 8, events), F32)], axis=0
    )
    cols = padded.T
    lane_e = lanes_of((events, LANES))
    sub_e = subs_of((LANES, events))
    tri_low = (lanes_of((events, events)) < subs_of((events, events))).astype(F32).astype(BF16)
    tri_up = (subs_of((events, events)) < lanes_of((events, events))).astype(F32).astype(BF16)

    hit_col, pos_col, slot_col, slot_row = [], [], [], []
    req_hi = jnp.zeros((LANES, LANES), F32)
    req_lo = jnp.zeros((LANES, LANES), F32)
    for side in range(2):
        owner_c = cols[:, side : side + 1].astype(jnp.int32)
        row_c = cols[:, 2 + side : 3 + side].astype(jnp.int32)
        hit_c = (owner_c == lane_e).astype(F32)
        hit_cb = hit_c.astype(BF16)
        pos_c = jnp.sum(mm(tri_low, hit_cb) * hit_c, axis=1, keepdims=True).astype(jnp.int32)
        pos_c = pos_c + side * cap
        owner_r = ints[side : side + 1, :]
        hit_r = (owner_r == sub_e).astype(F32)
        hit_rb = hit_r.astype(BF16)
        pos_r = jnp.sum(mm(hit_rb, tri_up) * hit_r, axis=0, keepdims=True).astype(jnp.int32)
        pos_r = pos_r + side * cap
        place = pos_c == lane_e % slots
        req_hi += mm(hit_rb, jnp.where(place, (row_c // 64 + 1).astype(F32), 0.0).astype(BF16))
        req_lo += mm(hit_rb, jnp.where(place, (row_c % 64).astype(F32), 0.0).astype(BF16))
        hit_col.append(hit_cb)
        pos_col.append(pos_c)
        slot_col.append(owner_c * slots + pos_c)
        slot_row.append(owner_r * slots + pos_r)
    request = jnp.where(req_hi > 0.5, (req_hi - 1.0) * 64.0 + req_lo, -1.0).astype(jnp.int32)
    for j in range(n):
        req_send[j] = request[j : j + 1, :]

    pl.semaphore_wait(barrier, n - 1)

    def send(phase, src, dst, device):
        return pltpu.make_async_remote_copy(
            src_ref=src,
            dst_ref=dst,
            send_sem=send_sems.at[phase],
            recv_sem=recv_sems.at[phase],
            device_id=coords(device),
            device_id_type=MESH,
        )

    def drain(sem, buf):
        part = buf.at[pl.ds(0, n - 1)]
        pltpu.make_async_copy(part, part, sem).wait()

    @pl.loop(1, n)
    def _(step):
        peer = (me + step) % n
        send(0, req_send.at[peer], req_recv.at[me], peer).start()

    for side in range(2):
        for g in range(groups):
            near = slot_col[side] == lanes_of((events, 256)) + g * 256
            pick_ref[side, :, g * 256 : (g + 1) * 256] = near.astype(F32).astype(BF16)

    req_recv[pl.ds(me, 1)] = req_send[pl.ds(me, 1)]
    drain(recv_sems.at[0], req_recv)

    lane_1 = lanes_of((1, LANES))
    blocks = []
    for b in range(n // rep):
        block = req_recv[b * rep]
        for q in range(1, rep):
            block = jnp.where(lane_1 // slots == q, req_recv[b * rep + q], block)
        blocks.append(block)
    flat = jnp.concatenate(blocks, axis=1)
    for g in range(groups):
        flat_ref[g] = flat[:, g * 256 : (g + 1) * 256]
    square = jnp.concatenate(
        [req_recv[j].astype(F32) for j in range(n)]
        + ([jnp.zeros((LANES - n, LANES), F32)] if n < LANES else []),
        axis=0,
    ).T.astype(jnp.int32)
    for j in range(n):
        rows_col[j * slots : (j + 1) * slots, :] = square[:slots, j : j + 1]

    for load in loads[5:]:
        load.wait()

    def serve(step):
        g = mirrored(step)
        wanted = rows_col[pl.ds(pl.multiple_of(g * 256, 256), 256), :]
        acc = jnp.zeros((256, width), F32)
        depth = 1024
        for k in range(rows_count // depth):
            onehot = (wanted == lanes_of((256, depth)) + k * depth).astype(F32).astype(BF16)
            acc += mm(onehot, mem_ref[k * depth : (k + 1) * depth, :])
        row_send[pl.ds(g * group, group)] = acc.astype(BF16).reshape(group, slots, width)
        for t in range(group):
            peer = g * group + (me + t) % group

            @pl.when(peer != me)
            def _():
                send(1, row_send.at[peer], row_recv.at[me], peer).start()

    serve(0)
    last = last_ref[...]
    high_count = rows_count // LANES
    last_hi = (last // 64).astype(F32)
    last_lo = (last % 64).astype(F32)
    fill = jnp.zeros((LANES - high_count, LANES), F32)
    table_hi = jnp.concatenate([last_hi, fill], axis=0).T.astype(BF16)
    table_lo = jnp.concatenate([last_lo, fill], axis=0).T.astype(BF16)
    onehot_hi = (flat // LANES == subs_of((LANES, total))).astype(F32).astype(BF16)
    found = mm(table_hi, onehot_hi) * 64.0 + mm(table_lo, onehot_hi)
    kept = jnp.where(flat % LANES == subs_of((LANES, total)), found, 0.0)
    picked_last = jnp.sum(kept, axis=0, keepdims=True).astype(jnp.int32)
    for b in range(n // rep):
        last_send[b] = picked_last[:, b * LANES : (b + 1) * LANES]

    @pl.loop(1, n)
    def _(step):
        peer = (me + step) % n
        send(2, last_send.at[peer // rep], last_recv.at[me], peer).start()

    pl.loop(1, groups)(serve)
    last_recv[pl.ds(me, 1)] = last_send[pl.ds(me // rep, 1)]
    row_recv[pl.ds(me, 1)] = row_send[pl.ds(me, 1)]

    edge_part = mm(edge_ref[...], win_ref[2 * width + time_width :, :]) + bmsg_ref[...]
    chunk = 512

    @pl.loop(0, rows_count // chunk)
    def _(step):
        base = pl.multiple_of(step * chunk, chunk)
        tally = jnp.zeros((chunk, 256), F32)
        for g in range(groups):
            hits = (flat_ref[g] == subs_of((chunk, 256)) + base).astype(F32)
            hits_ref[g, pl.ds(base, chunk), :] = hits.astype(BF16)
            tally += hits
        count_ref[pl.ds(base, chunk), :] = jnp.sum(tally, axis=1, keepdims=True)
        state_ref[pl.ds(base, chunk), :] = mm(mem_ref[pl.ds(base, chunk), :], ghid_ref[...])


    slot_both = jnp.concatenate(slot_row, axis=1)

    @pl.loop(0, groups)
    def _(g):
        placed = slot_both == subs_of((256, 2 * events)) + g * 256
        place_ref[g] = placed.astype(F32).astype(BF16)

    drain(recv_sems.at[2], last_recv)
    got = jnp.concatenate(
        [last_recv[j] for j in range(n)]
        + ([jnp.zeros((LANES - n, LANES), jnp.int32)] if n < LANES else []),
        axis=0,
    )
    got_hi = (got // 64).astype(F32).astype(BF16)
    got_lo = (got % 64).astype(F32).astype(BF16)
    moment = cols[:, 4:5]
    coded = []
    for side in range(2):
        spread = mm(hit_col[side], got_hi) * 64.0 + mm(hit_col[side], got_lo)
        here = pos_col[side] + (me % rep) * slots == lane_e
        before = jnp.sum(jnp.where(here, spread, 0.0), axis=1, keepdims=True)
        angle = (moment - before) * freq_ref[...] + phase_ref[...]
        coded.append(jnp.cos(angle).astype(BF16))

    drain(recv_sems.at[1], row_recv)
    fetched = row_recv[...].reshape(total, width)
    picked = []
    for side in range(2):
        picked.append(mm(pick_ref[side], fetched).astype(BF16))
    for side in range(2):
        inputs = jnp.concatenate([picked[side], picked[1 - side], coded[side]], axis=1)
        hid = mm(inputs, win_ref[: 2 * width + time_width, :]) + edge_part
        hid = jnp.maximum(hid, 0.0).astype(BF16)
        msgs[side * events : (side + 1) * events, :] = mm(hid, wout_ref[...]).astype(BF16)


    def push(first, stop, kind):
        @pl.loop(first, stop)
        def _(step):
            g = mirrored(step)
            block = mm(place_ref[g], msgs[...])
            msg_send[pl.ds(g * group, group)] = block.astype(BF16).reshape(
                group, slots, block.shape[1]
            )
            for t in range(group):
                peer = g * group + (me + t) % group

                @pl.when(peer != me)
                def _():
                    send(kind, msg_send.at[peer], msg_recv.at[me], peer).start()

    half, quarter = groups // 2, groups // 4
    push(0, quarter, 3)
    push(quarter, half, 4)
    push(half, groups, 5)
    msg_recv[pl.ds(me, 1)] = msg_send[pl.ds(me, 1)]
    drain(send_sems.at[0], req_send)
    drain(send_sems.at[1], row_send)
    drain(send_sems.at[2], last_recv)

    def settle(sem, buf, blocks_moved):
        part = buf.at[pl.ds(0, blocks_moved)]
        pltpu.make_async_copy(part, part, sem).wait()

    def gathered(base, steps):
        acc = jnp.zeros((chunk, msgs.shape[1]), F32)
        for step in steps:
            g = mirrored(step)
            block = msg_recv[pl.ds(g * group, group)].reshape(256, msgs.shape[1])
            acc += mm(hits_ref[g, pl.ds(base, chunk), :], block)
        return acc

    settle(recv_sems.at[5], msg_recv, half * group - 1)

    @pl.loop(0, rows_count // chunk)
    def _(step):
        base = pl.multiple_of(step * chunk, chunk)
        sum_ref[pl.ds(base, chunk), :] = gathered(base, range(half, groups))

    settle(recv_sems.at[3], msg_recv, quarter * group)

    @pl.loop(0, rows_count // chunk)
    def _(step):
        base = pl.multiple_of(step * chunk, chunk)
        sum_ref[pl.ds(base, chunk), :] += gathered(base, range(quarter))

    settle(recv_sems.at[4], msg_recv, (half - quarter) * group)

    @pl.loop(0, rows_count // chunk)
    def _(step):
        base = pl.multiple_of(step * chunk, chunk)
        rows = pl.ds(base, chunk)
        count = count_ref[rows, :]
        summed = sum_ref[rows, :] + gathered(base, range(quarter, half))
        mean = (summed / jnp.maximum(count, 1.0)).astype(BF16)
        state = mem_ref[rows, :].astype(F32)
        gi = mm(mean, gin_ref[...]) + bgru_ref[...]
        gh = state_ref[rows, :]
        reset = 0.5 * jnp.tanh(0.5 * (gi[:, :width] + gh[:, :width])) + 0.5
        update = 0.5 * jnp.tanh(0.5 * (gi[:, width : 2 * width] + gh[:, width : 2 * width])) + 0.5
        candid = jnp.tanh(gi[:, 2 * width :] + reset * gh[:, 2 * width :])
        fresh = candid + update * (state - candid)
        out_ref[rows, :] = jnp.where(count > 0.5, fresh, state).astype(BF16)
        pltpu.make_async_copy(out_ref.at[rows], out_hbm.at[rows], store_sem).start()

    settle(send_sems.at[3], msg_send, quarter * group)
    settle(send_sems.at[4], msg_send, (half - quarter) * group)
    settle(send_sems.at[5], msg_send, half * group - 1)
    pltpu.make_async_copy(out_ref, out_hbm, store_sem).wait()


def local(
    per_row,
    src_owner,
    src_row,
    dst_owner,
    dst_row,
    event_time,
    edge_feat,
    memory,
    last_update,
    time_freq,
    time_phase,
    w_msg_in,
    b_msg,
    w_msg_out,
    w_gru_in,
    b_gru_in,
    w_gru_hid,
):
    n = lax.axis_size(("ev", "node"))
    events = edge_feat.shape[0]
    slots = 2 * max(2, 2 * events // n)
    rows_count, width = memory.shape
    msg_width = w_msg_out.shape[1]
    total = n * slots
    operands = (
        src_owner.reshape(1, events),
        dst_owner.reshape(1, events),
        src_row.reshape(1, events),
        dst_row.reshape(1, events),
        event_time.reshape(1, events),
        time_freq.reshape(1, -1),
        time_phase.reshape(1, -1),
        b_msg.reshape(1, -1),
        b_gru_in.reshape(1, -1),
        last_update.reshape(rows_count // LANES, LANES),
        memory,
        edge_feat,
        w_msg_in,
        w_msg_out,
        w_gru_in,
        w_gru_hid,
    )
    anywhere = pl.BlockSpec(memory_space=pl.ANY)
    return pl.pallas_call(
        functools.partial(exchange_kernel, n, per_row, slots, events, time_freq.shape[0]),
        out_shape=jax.ShapeDtypeStruct(memory.shape, BF16),
        in_specs=[anywhere] * len(operands),
        out_specs=anywhere,
        scratch_shapes=[pltpu.VMEM(x.shape, x.dtype) for x in operands]
        + [
            pltpu.VMEM(memory.shape, BF16),
            pltpu.VMEM((n, 1, LANES), jnp.int32),
            pltpu.VMEM((n, 1, LANES), jnp.int32),
            pltpu.VMEM((total, 1), jnp.int32),
            pltpu.VMEM((2, events, total), BF16),
            pltpu.VMEM((total // 256, 256, 2 * events), BF16),
            pltpu.VMEM((n * slots // LANES, 1, LANES), jnp.int32),
            pltpu.VMEM((n, 1, LANES), jnp.int32),
            pltpu.VMEM((n, slots, width), BF16),
            pltpu.VMEM((n, slots, width), BF16),
            pltpu.VMEM((n, slots, msg_width), BF16),
            pltpu.VMEM((n, slots, msg_width), BF16),
            pltpu.VMEM((2 * events, msg_width), BF16),
            pltpu.VMEM((total // 256, 1, 256), jnp.int32),
            pltpu.VMEM((total // 256, rows_count, 256), BF16),
            pltpu.VMEM((rows_count, 1), F32),
            pltpu.VMEM((rows_count, 3 * width), F32),
            pltpu.VMEM((rows_count, msg_width), F32),
            pltpu.SemaphoreType.DMA((6,)),
            pltpu.SemaphoreType.DMA((6,)),
            pltpu.SemaphoreType.DMA((len(operands),)),
            pltpu.SemaphoreType.DMA,
        ],
        compiler_params=pltpu.CompilerParams(
            collective_id=0, has_side_effects=True, vmem_limit_bytes=60 * 1024 * 1024
        ),
        name="exchange",
    )(*operands)


def solution(mesh):
    in_specs = (
        P(("ev", "node"), None),
        P(("ev", "node")),
        P(("ev", "node"), None),
        P(("ev", "node")),
        P(("ev", "node")),
        P(("ev", "node"), None),
        P(("ev", "node"), None),
        P(("ev", "node")),
        P(),
        P(),
        P(),
        P(),
        P(),
        P(),
        P(),
        P(),
    )
    out_specs = P(("ev", "node"), None)
    return jax.shard_map(
        functools.partial(local, mesh.shape["node"]),
        mesh=mesh,
        in_specs=in_specs,
        out_specs=out_specs,
        check_vma=False,
    )
```

```python
import functools

import jax
import jax.numpy as jnp
from jax import lax
from jax.experimental import pallas as pl
from jax.experimental.pallas import tpu as pltpu
from jax.sharding import PartitionSpec as P

MESH = pl.DeviceIdType.MESH
LANES = 128
F32 = jnp.float32
BF16 = jnp.bfloat16


def mm(a, b):
    return jnp.dot(a, b, preferred_element_type=F32)


def lanes_of(shape):
    return lax.broadcasted_iota(jnp.int32, shape, 1)


def subs_of(shape):
    return lax.broadcasted_iota(jnp.int32, shape, 0)


def exchange_kernel(
    n,
    per_row,
    slots,
    events,
    time_width,
    so_hbm,
    do_hbm,
    sr_hbm,
    dr_hbm,
    et_hbm,
    freq_hbm,
    phase_hbm,
    bmsg_hbm,
    bgru_hbm,
    last_hbm,
    mem_hbm,
    edge_hbm,
    win_hbm,
    wout_hbm,
    gin_hbm,
    ghid_hbm,
    out_hbm,
    so_ref,
    do_ref,
    sr_ref,
    dr_ref,
    et_ref,
    freq_ref,
    phase_ref,
    bmsg_ref,
    bgru_ref,
    last_ref,
    mem_ref,
    edge_ref,
    win_ref,
    wout_ref,
    gin_ref,
    ghid_ref,
    out_ref,
    req_send,
    req_recv,
    rows_col,
    pick_ref,
    place_ref,
    pick_sum,
    last_send,
    last_recv,
    row_send,
    row_recv,
    msg_send,
    msg_recv,
    msgs,
    flat_ref,
    hits_ref,
    scale_ref,
    state_ref,
    sum_ref,
    send_sems,
    recv_sems,
    load_sems,
    store_sem,
):
    ev = lax.axis_index("ev")
    me = ev * per_row + lax.axis_index("node")
    rows_count, width = mem_ref.shape
    hidden = wout_ref.shape[0]
    cap = slots // 2
    rep = LANES // slots
    total = n * slots
    group = 256 // slots
    groups = n // group

    def coords(device):
        return (device // per_row, device % per_row)

    half = groups // 2
    quarter = half - 1

    def mirrored(step):
        k = (step + groups // 2) % groups
        k = k + (step // (groups // 2)) * (groups // 2 - 1 - 2 * k)
        g, unit = 0, 1
        while unit < groups:
            g = g + unit * ((me // group // unit + k // unit) % 2)
            unit = 2 * unit
        return g

    barrier = pltpu.get_barrier_semaphore()

    loads = [
        pltpu.make_async_copy(src, dst, load_sems.at[k])
        for k, (src, dst) in enumerate(
            [
                (so_hbm, so_ref),
                (do_hbm, do_ref),
                (sr_hbm, sr_ref),
                (dr_hbm, dr_ref),
                (et_hbm, et_ref),
                (last_hbm, last_ref),
                (freq_hbm, freq_ref),
                (phase_hbm, phase_ref),
                (bmsg_hbm, bmsg_ref),
                (bgru_hbm, bgru_ref),
                (mem_hbm, mem_ref),
                (edge_hbm, edge_ref),
                (win_hbm, win_ref),
                (wout_hbm, wout_ref),
                (ghid_hbm, ghid_ref),
                (gin_hbm, gin_ref),
            ]
        )
    ]
    for load in loads:
        load.start()
    @pl.loop(1, n)
    def _(step):
        pl.semaphore_signal(
            barrier, inc=1, device_id=coords((me + step) % n), device_id_type=MESH
        )

    for load in loads[:5]:
        load.wait()
    ints = jnp.concatenate(
        [so_ref[...], do_ref[...], sr_ref[...], dr_ref[...], et_ref[...]]
        + [jnp.zeros((3, events), jnp.int32)],
        axis=0,
    )
    padded = jnp.concatenate(
        [ints.astype(F32), jnp.zeros((LANES - 8, events), F32)], axis=0
    )
    cols = padded.T
    lane_e = lanes_of((events, LANES))
    sub_e = subs_of((LANES, events))
    tri_low = (lanes_of((events, events)) < subs_of((events, events))).astype(F32).astype(BF16)
    tri_up = (subs_of((events, events)) < lanes_of((events, events))).astype(F32).astype(BF16)

    hit_col, pos_col, slot_col, slot_row = [], [], [], []
    req_hi = jnp.zeros((LANES, LANES), F32)
    req_lo = jnp.zeros((LANES, LANES), F32)
    for side in range(2):
        owner_c = cols[:, side : side + 1].astype(jnp.int32)
        row_c = cols[:, 2 + side : 3 + side].astype(jnp.int32)
        hit_c = (owner_c == lane_e).astype(F32)
        hit_cb = hit_c.astype(BF16)
        pos_c = jnp.sum(mm(tri_low, hit_cb) * hit_c, axis=1, keepdims=True).astype(jnp.int32)
        pos_c = pos_c + side * cap
        owner_r = ints[side : side + 1, :]
        hit_r = (owner_r == sub_e).astype(F32)
        hit_rb = hit_r.astype(BF16)
        pos_r = jnp.sum(mm(hit_rb, tri_up) * hit_r, axis=0, keepdims=True).astype(jnp.int32)
        pos_r = pos_r + side * cap
        place = pos_c == lane_e % slots
        req_hi += mm(hit_rb, jnp.where(place, (row_c // 64 + 1).astype(F32), 0.0).astype(BF16))
        req_lo += mm(hit_rb, jnp.where(place, (row_c % 64).astype(F32), 0.0).astype(BF16))
        hit_col.append(hit_cb)
        pos_col.append(pos_c)
        slot_col.append(owner_c * slots + pos_c)
        slot_row.append(owner_r * slots + pos_r)
    request = jnp.where(req_hi > 0.5, (req_hi - 1.0) * 64.0 + req_lo, -1.0).astype(jnp.int32)
    for j in range(n):
        req_send[j] = request[j : j + 1, :]

    pl.semaphore_wait(barrier, n - 1)

    def send(phase, src, dst, device):
        return pltpu.make_async_remote_copy(
            src_ref=src,
            dst_ref=dst,
            send_sem=send_sems.at[phase],
            recv_sem=recv_sems.at[phase],
            device_id=coords(device),
            device_id_type=MESH,
        )

    def drain(sem, buf):
        part = buf.at[pl.ds(0, n - 1)]
        pltpu.make_async_copy(part, part, sem).wait()

    @pl.loop(1, n)
    def _(step):
        peer = (me + step) % n
        send(0, req_send.at[peer], req_recv.at[me], peer).start()

    for side in range(2):
        for g in range(groups):
            near = slot_col[side] == lanes_of((events, 256)) + g * 256
            pick_ref[g, side * events : (side + 1) * events, :] = near.astype(F32).astype(BF16)

    req_recv[pl.ds(me, 1)] = req_send[pl.ds(me, 1)]
    drain(recv_sems.at[0], req_recv)

    lane_1 = lanes_of((1, LANES))
    blocks = []
    for b in range(n // rep):
        block = req_recv[b * rep]
        for q in range(1, rep):
            block = jnp.where(lane_1 // slots == q, req_recv[b * rep + q], block)
        blocks.append(block)
    flat = jnp.concatenate(blocks, axis=1)
    for g in range(groups):
        flat_ref[g] = flat[:, g * 256 : (g + 1) * 256]
    square = jnp.concatenate(
        [req_recv[j].astype(F32) for j in range(n)]
        + ([jnp.zeros((LANES - n, LANES), F32)] if n < LANES else []),
        axis=0,
    ).T.astype(jnp.int32)
    for j in range(n):
        rows_col[j * slots : (j + 1) * slots, :] = square[:slots, j : j + 1]

    for load in loads[5:]:
        load.wait()

    def serve(kind, step):
        g = mirrored(step)
        wanted = rows_col[pl.ds(pl.multiple_of(g * 256, 256), 256), :]
        acc = jnp.zeros((256, width), F32)
        depth = 1024
        for k in range(rows_count // depth):
            onehot = (wanted == lanes_of((256, depth)) + k * depth).astype(F32).astype(BF16)
            acc += mm(onehot, mem_ref[k * depth : (k + 1) * depth, :])
        row_send[pl.ds(g * group, group)] = acc.astype(BF16).reshape(group, slots, width)
        for t in range(group):
            peer = g * group + (me + t) % group

            @pl.when(peer != me)
            def _():
                send(kind, row_send.at[peer], row_recv.at[me], peer).start()

    serve(1, 0)
    last = last_ref[...]
    high_count = rows_count // LANES
    last_hi = (last // 64).astype(F32)
    last_lo = (last % 64).astype(F32)
    fill = jnp.zeros((LANES - high_count, LANES), F32)
    table_hi = jnp.concatenate([last_hi, fill], axis=0).T.astype(BF16)
    table_lo = jnp.concatenate([last_lo, fill], axis=0).T.astype(BF16)
    onehot_hi = (flat // LANES == subs_of((LANES, total))).astype(F32).astype(BF16)
    found = mm(table_hi, onehot_hi) * 64.0 + mm(table_lo, onehot_hi)
    kept = jnp.where(flat % LANES == subs_of((LANES, total)), found, 0.0)
    picked_last = jnp.sum(kept, axis=0, keepdims=True).astype(jnp.int32)
    for b in range(n // rep):
        last_send[b] = picked_last[:, b * LANES : (b + 1) * LANES]

    @pl.loop(1, n)
    def _(step):
        peer = (me + step) % n
        send(2, last_send.at[peer // rep], last_recv.at[me], peer).start()

    pl.loop(1, half)(functools.partial(serve, 1))
    pl.loop(half, groups)(functools.partial(serve, 6))
    last_recv[pl.ds(me, 1)] = last_send[pl.ds(me // rep, 1)]
    row_recv[pl.ds(me, 1)] = row_send[pl.ds(me, 1)]

    edge_part = mm(edge_ref[...], win_ref[2 * width + time_width :, :]) + bmsg_ref[...]
    chunk = 512

    @pl.loop(0, rows_count // chunk)
    def _(step):
        base = pl.multiple_of(step * chunk, chunk)
        tally = jnp.zeros((chunk, 256), F32)
        for g in range(groups):
            hits = (flat_ref[g] == subs_of((chunk, 256)) + base).astype(F32)
            hits_ref[g, pl.ds(base, chunk), :] = hits.astype(BF16)
            tally += hits
        count = jnp.sum(tally, axis=1, keepdims=True)
        scale_ref[pl.ds(base, chunk), :] = jnp.where(count > 0.5, 1.0 / jnp.maximum(count, 1.0), -1.0)
        state_ref[pl.ds(base, chunk), :] = mm(mem_ref[pl.ds(base, chunk), :], ghid_ref[...])


    slot_both = jnp.concatenate(slot_row, axis=1)

    @pl.loop(0, groups)
    def _(g):
        placed = slot_both == subs_of((256, 2 * events)) + g * 256
        place_ref[g] = placed.astype(F32).astype(BF16)

    drain(recv_sems.at[2], last_recv)
    got = jnp.concatenate(
        [last_recv[j] for j in range(n)]
        + ([jnp.zeros((LANES - n, LANES), jnp.int32)] if n < LANES else []),
        axis=0,
    )
    got_hi = (got // 64).astype(F32).astype(BF16)
    got_lo = (got % 64).astype(F32).astype(BF16)
    moment = cols[:, 4:5]
    coded = []
    for side in range(2):
        spread = mm(hit_col[side], got_hi) * 64.0 + mm(hit_col[side], got_lo)
        here = pos_col[side] + (me % rep) * slots == lane_e
        before = jnp.sum(jnp.where(here, spread, 0.0), axis=1, keepdims=True)
        angle = (moment - before) * freq_ref[...] + phase_ref[...]
        coded.append(jnp.cos(angle).astype(BF16))

    def settle(sem, buf, blocks_moved):
        part = buf.at[pl.ds(0, blocks_moved)]
        pltpu.make_async_copy(part, part, sem).wait()

    def chosen(steps):
        acc = jnp.zeros((2 * events, width), F32)
        for step in steps:
            g = mirrored(step)
            block = row_recv[pl.ds(g * group, group)].reshape(256, width)
            acc += mm(pick_ref[g], block)
        return acc

    settle(recv_sems.at[6], row_recv, half * group - 1)
    pick_sum[...] = chosen(range(half, groups))
    settle(recv_sems.at[1], row_recv, half * group)
    both = (pick_sum[...] + chosen(range(half))).astype(BF16)
    picked = [both[:events], both[events:]]
    for side in range(2):
        inputs = jnp.concatenate([picked[side], picked[1 - side], coded[side]], axis=1)
        hid = mm(inputs, win_ref[: 2 * width + time_width, :]) + edge_part
        hid = jnp.maximum(hid, 0.0).astype(BF16)
        msgs[side * events : (side + 1) * events, :] = mm(hid, wout_ref[...]).astype(BF16)


    def push(first, stop, kind):
        @pl.loop(first, stop)
        def _(step):
            g = mirrored(step)
            block = mm(place_ref[g], msgs[...])
            msg_send[pl.ds(g * group, group)] = block.astype(BF16).reshape(
                group, slots, block.shape[1]
            )
            for t in range(group):
                peer = g * group + (me + t) % group

                @pl.when(peer != me)
                def _():
                    send(kind, msg_send.at[peer], msg_recv.at[me], peer).start()

    push(0, quarter, 3)
    push(quarter, half, 4)
    push(half, groups, 5)
    msg_recv[pl.ds(me, 1)] = msg_send[pl.ds(me, 1)]
    drain(send_sems.at[0], req_send)
    settle(send_sems.at[1], row_send, half * group)
    settle(send_sems.at[6], row_send, half * group - 1)
    drain(send_sems.at[2], last_recv)

    def gathered(base, steps):
        acc = jnp.zeros((chunk, msgs.shape[1]), F32)
        for step in steps:
            g = mirrored(step)
            block = msg_recv[pl.ds(g * group, group)].reshape(256, msgs.shape[1])
            acc += mm(hits_ref[g, pl.ds(base, chunk), :], block)
        return acc

    settle(recv_sems.at[5], msg_recv, half * group - 1)

    @pl.loop(0, rows_count // chunk)
    def _(step):
        base = pl.multiple_of(step * chunk, chunk)
        sum_ref[pl.ds(base, chunk), :] = gathered(base, range(half, groups))

    settle(recv_sems.at[3], msg_recv, quarter * group)

    @pl.loop(0, rows_count // chunk)
    def _(step):
        base = pl.multiple_of(step * chunk, chunk)
        sum_ref[pl.ds(base, chunk), :] += gathered(base, range(quarter))

    settle(recv_sems.at[4], msg_recv, (half - quarter) * group)

    @pl.loop(0, rows_count // chunk)
    def _(step):
        base = pl.multiple_of(step * chunk, chunk)
        rows = pl.ds(base, chunk)
        scale = scale_ref[rows, :]
        summed = sum_ref[rows, :] + gathered(base, range(quarter, half))
        mean = (summed * scale).astype(BF16)
        state = mem_ref[rows, :].astype(F32)
        gi = mm(mean, gin_ref[...]) + bgru_ref[...].reshape(1, 3 * width)
        gh = state_ref[rows, :]
        reset = 0.5 * jnp.tanh(0.5 * (gi[:, :width] + gh[:, :width])) + 0.5
        update = 0.5 * jnp.tanh(0.5 * (gi[:, width : 2 * width] + gh[:, width : 2 * width])) + 0.5
        candid = jnp.tanh(gi[:, 2 * width :] + reset * gh[:, 2 * width :])
        fresh = candid + update * (state - candid)
        out_ref[rows, :] = jnp.where(scale > 0.0, fresh, state).astype(BF16)
        pltpu.make_async_copy(out_ref.at[rows], out_hbm.at[rows], store_sem).start()

    settle(send_sems.at[3], msg_send, quarter * group)
    settle(send_sems.at[4], msg_send, (half - quarter) * group)
    settle(send_sems.at[5], msg_send, half * group - 1)
    pltpu.make_async_copy(out_ref, out_hbm, store_sem).wait()


def hand_over_kernel(in_ref, out_ref):
    out_ref[...] = in_ref[...]


def local(
    per_row,
    src_owner,
    src_row,
    dst_owner,
    dst_row,
    event_time,
    edge_feat,
    memory,
    last_update,
    time_freq,
    time_phase,
    w_msg_in,
    b_msg,
    w_msg_out,
    w_gru_in,
    b_gru_in,
    w_gru_hid,
):
    n = lax.axis_size(("ev", "node"))
    events = edge_feat.shape[0]
    slots = 2 * max(2, 2 * events // n)
    rows_count, width = memory.shape
    msg_width = w_msg_out.shape[1]
    total = n * slots
    operands = (
        src_owner.reshape(1, events),
        dst_owner.reshape(1, events),
        src_row.reshape(1, events),
        dst_row.reshape(1, events),
        event_time.reshape(1, events),
        time_freq.reshape(1, -1),
        time_phase.reshape(1, -1),
        b_msg.reshape(1, -1),
        b_gru_in,
        last_update.reshape(rows_count // LANES, LANES),
        memory,
        edge_feat,
        w_msg_in,
        w_msg_out,
        w_gru_in,
        w_gru_hid,
    )
    anywhere = pl.BlockSpec(memory_space=pl.ANY)
    result = pl.pallas_call(
        functools.partial(exchange_kernel, n, per_row, slots, events, time_freq.shape[0]),
        out_shape=jax.ShapeDtypeStruct(memory.shape, BF16),
        in_specs=[anywhere] * len(operands),
        out_specs=anywhere,
        scratch_shapes=[pltpu.VMEM(x.shape, x.dtype) for x in operands]
        + [
            pltpu.VMEM(memory.shape, BF16),
            pltpu.VMEM((n, 1, LANES), jnp.int32),
            pltpu.VMEM((n, 1, LANES), jnp.int32),
            pltpu.VMEM((total, 1), jnp.int32),
            pltpu.VMEM((total // 256, 2 * events, 256), BF16),
            pltpu.VMEM((total // 256, 256, 2 * events), BF16),
            pltpu.VMEM((2 * events, width), F32),
            pltpu.VMEM((n * slots // LANES, 1, LANES), jnp.int32),
            pltpu.VMEM((n, 1, LANES), jnp.int32),
            pltpu.VMEM((n, slots, width), BF16),
            pltpu.VMEM((n, slots, width), BF16),
            pltpu.VMEM((n, slots, msg_width), BF16),
            pltpu.VMEM((n, slots, msg_width), BF16),
            pltpu.VMEM((2 * events, msg_width), BF16),
            pltpu.VMEM((total // 256, 1, 256), jnp.int32),
            pltpu.VMEM((total // 256, rows_count, 256), BF16),
            pltpu.VMEM((rows_count, 1), F32),
            pltpu.VMEM((rows_count, 3 * width), F32),
            pltpu.VMEM((rows_count, msg_width), F32),
            pltpu.SemaphoreType.DMA((7,)),
            pltpu.SemaphoreType.DMA((7,)),
            pltpu.SemaphoreType.DMA((len(operands),)),
            pltpu.SemaphoreType.DMA,
        ],
        compiler_params=pltpu.CompilerParams(
            collective_id=0, has_side_effects=True, vmem_limit_bytes=60 * 1024 * 1024
        ),
        name="exchange",
    )(*operands)
    part = pl.BlockSpec((min(1024, rows_count), width), lambda i: (i, 0))
    return pl.pallas_call(
        hand_over_kernel,
        grid=(rows_count // min(1024, rows_count),),
        out_shape=jax.ShapeDtypeStruct(memory.shape, BF16),
        in_specs=[part],
        out_specs=part,
        compiler_params=pltpu.CompilerParams(vmem_limit_bytes=60 * 1024 * 1024),
        name="hand_over",
    )(result)


def solution(mesh):
    in_specs = (
        P(("ev", "node"), None),
        P(("ev", "node")),
        P(("ev", "node"), None),
        P(("ev", "node")),
        P(("ev", "node")),
        P(("ev", "node"), None),
        P(("ev", "node"), None),
        P(("ev", "node")),
        P(),
        P(),
        P(),
        P(),
        P(),
        P(),
        P(),
        P(),
    )
    out_specs = P(("ev", "node"), None)
    return jax.shard_map(
        functools.partial(local, mesh.shape["node"]),
        mesh=mesh,
        in_specs=in_specs,
        out_specs=out_specs,
        check_vma=False,
    )
```

```python
import functools

import jax
import jax.numpy as jnp
from jax import lax
from jax.experimental import pallas as pl
from jax.experimental.pallas import tpu as pltpu
from jax.sharding import PartitionSpec as P

MESH = pl.DeviceIdType.MESH
LANES = 128
F32 = jnp.float32
BF16 = jnp.bfloat16


def mm(a, b):
    return jnp.dot(a, b, preferred_element_type=F32)


def lanes_of(shape):
    return lax.broadcasted_iota(jnp.int32, shape, 1)


def subs_of(shape):
    return lax.broadcasted_iota(jnp.int32, shape, 0)


def exchange_kernel(
    n,
    per_row,
    slots,
    events,
    time_width,
    so_hbm,
    do_hbm,
    sr_hbm,
    dr_hbm,
    et_hbm,
    freq_hbm,
    phase_hbm,
    bmsg_hbm,
    bgru_hbm,
    last_hbm,
    mem_hbm,
    edge_hbm,
    win_hbm,
    wout_hbm,
    gin_hbm,
    ghid_hbm,
    out_hbm,
    so_ref,
    do_ref,
    sr_ref,
    dr_ref,
    et_ref,
    freq_ref,
    phase_ref,
    bmsg_ref,
    bgru_ref,
    last_ref,
    mem_ref,
    edge_ref,
    win_ref,
    wout_ref,
    gin_ref,
    ghid_ref,
    out_ref,
    req_send,
    req_recv,
    rows_col,
    pick_ref,
    place_ref,
    pick_sum,
    last_send,
    last_recv,
    row_send,
    row_recv,
    msg_send,
    msg_recv,
    msgs,
    flat_ref,
    hits_ref,
    scale_ref,
    state_ref,
    sum_ref,
    send_sems,
    recv_sems,
    load_sems,
    store_sem,
):
    ev = lax.axis_index("ev")
    me = ev * per_row + lax.axis_index("node")
    rows_count, width = mem_ref.shape
    hidden = wout_ref.shape[0]
    cap = slots // 2
    rep = LANES // slots
    total = n * slots
    group = 256 // slots
    groups = n // group

    def coords(device):
        return (device // per_row, device % per_row)

    half = groups // 2
    quarter = half - 1

    def mirrored(step):
        k = (step + groups // 2) % groups
        k = k + (step // (groups // 2)) * (groups // 2 - 1 - 2 * k)
        g, unit = 0, 1
        while unit < groups:
            g = g + unit * ((me // group // unit + k // unit) % 2)
            unit = 2 * unit
        return g

    barrier = pltpu.get_barrier_semaphore()

    loads = [
        pltpu.make_async_copy(src, dst, load_sems.at[k])
        for k, (src, dst) in enumerate(
            [
                (so_hbm, so_ref),
                (do_hbm, do_ref),
                (sr_hbm, sr_ref),
                (dr_hbm, dr_ref),
                (et_hbm, et_ref),
                (last_hbm, last_ref),
                (freq_hbm, freq_ref),
                (phase_hbm, phase_ref),
                (bmsg_hbm, bmsg_ref),
                (bgru_hbm, bgru_ref),
                (mem_hbm, mem_ref),
                (edge_hbm, edge_ref),
                (win_hbm, win_ref),
                (wout_hbm, wout_ref),
                (ghid_hbm, ghid_ref),
                (gin_hbm, gin_ref),
            ]
        )
    ]
    for load in loads:
        load.start()
    @pl.loop(1, n)
    def _(step):
        pl.semaphore_signal(
            barrier, inc=1, device_id=coords((me + step) % n), device_id_type=MESH
        )

    for load in loads[:5]:
        load.wait()
    ints = jnp.concatenate(
        [so_ref[...], do_ref[...], sr_ref[...], dr_ref[...], et_ref[...]]
        + [jnp.zeros((3, events), jnp.int32)],
        axis=0,
    )
    padded = jnp.concatenate(
        [ints.astype(F32), jnp.zeros((LANES - 8, events), F32)], axis=0
    )
    cols = padded.T
    lane_e = lanes_of((events, LANES))
    sub_e = subs_of((LANES, events))
    tri_low = (lanes_of((events, events)) < subs_of((events, events))).astype(F32).astype(BF16)
    tri_up = (subs_of((events, events)) < lanes_of((events, events))).astype(F32).astype(BF16)

    hit_col, pos_col, slot_col, slot_row = [], [], [], []
    req_hi = jnp.zeros((LANES, LANES), F32)
    req_lo = jnp.zeros((LANES, LANES), F32)
    for side in range(2):
        owner_c = cols[:, side : side + 1].astype(jnp.int32)
        row_c = cols[:, 2 + side : 3 + side].astype(jnp.int32)
        hit_c = (owner_c == lane_e).astype(F32)
        hit_cb = hit_c.astype(BF16)
        pos_c = jnp.sum(mm(tri_low, hit_cb) * hit_c, axis=1, keepdims=True).astype(jnp.int32)
        pos_c = pos_c + side * cap
        owner_r = ints[side : side + 1, :]
        hit_r = (owner_r == sub_e).astype(F32)
        hit_rb = hit_r.astype(BF16)
        pos_r = jnp.sum(mm(hit_rb, tri_up) * hit_r, axis=0, keepdims=True).astype(jnp.int32)
        pos_r = pos_r + side * cap
        place = pos_c == lane_e % slots
        req_hi += mm(hit_rb, jnp.where(place, (row_c // 64 + 1).astype(F32), 0.0).astype(BF16))
        req_lo += mm(hit_rb, jnp.where(place, (row_c % 64).astype(F32), 0.0).astype(BF16))
        hit_col.append(hit_cb)
        pos_col.append(pos_c)
        slot_col.append(owner_c * slots + pos_c)
        slot_row.append(owner_r * slots + pos_r)
    request = jnp.where(req_hi > 0.5, (req_hi - 1.0) * 64.0 + req_lo, -1.0).astype(jnp.int32)
    for j in range(n):
        req_send[j] = request[j : j + 1, :]

    pl.semaphore_wait(barrier, n - 1)

    def send(phase, src, dst, device):
        return pltpu.make_async_remote_copy(
            src_ref=src,
            dst_ref=dst,
            send_sem=send_sems.at[phase],
            recv_sem=recv_sems.at[phase],
            device_id=coords(device),
            device_id_type=MESH,
        )

    def drain(sem, buf):
        part = buf.at[pl.ds(0, n - 1)]
        pltpu.make_async_copy(part, part, sem).wait()

    @pl.loop(1, n)
    def _(step):
        peer = (me + step) % n
        send(0, req_send.at[peer], req_recv.at[me], peer).start()

    for side in range(2):
        for g in range(groups):
            near = slot_col[side] == lanes_of((events, 256)) + g * 256
            pick_ref[g, side * events : (side + 1) * events, :] = near.astype(F32).astype(BF16)

    req_recv[pl.ds(me, 1)] = req_send[pl.ds(me, 1)]
    drain(recv_sems.at[0], req_recv)

    lane_1 = lanes_of((1, LANES))
    blocks = []
    for b in range(n // rep):
        block = req_recv[b * rep]
        for q in range(1, rep):
            block = jnp.where(lane_1 // slots == q, req_recv[b * rep + q], block)
        blocks.append(block)
    flat = jnp.concatenate(blocks, axis=1)
    for g in range(groups):
        flat_ref[g] = flat[:, g * 256 : (g + 1) * 256]
    square = jnp.concatenate(
        [req_recv[j].astype(F32) for j in range(n)]
        + ([jnp.zeros((LANES - n, LANES), F32)] if n < LANES else []),
        axis=0,
    ).T.astype(jnp.int32)
    for j in range(n):
        rows_col[j * slots : (j + 1) * slots, :] = square[:slots, j : j + 1]

    for load in loads[5:]:
        load.wait()

    def serve(kind, step):
        g = mirrored(step)
        wanted = rows_col[pl.ds(pl.multiple_of(g * 256, 256), 256), :]
        acc = jnp.zeros((256, width), F32)
        depth = 1024
        for k in range(rows_count // depth):
            onehot = (wanted == lanes_of((256, depth)) + k * depth).astype(F32).astype(BF16)
            acc += mm(onehot, mem_ref[k * depth : (k + 1) * depth, :])
        row_send[pl.ds(g * group, group)] = acc.astype(BF16).reshape(group, slots, width)
        for t in range(group):
            peer = g * group + (me + t) % group

            @pl.when(peer != me)
            def _():
                send(kind, row_send.at[peer], row_recv.at[me], peer).start()

    serve(1, 0)
    last = last_ref[...]
    high_count = rows_count // LANES
    last_hi = (last // 64).astype(F32)
    last_lo = (last % 64).astype(F32)
    fill = jnp.zeros((LANES - high_count, LANES), F32)
    table_hi = jnp.concatenate([last_hi, fill], axis=0).T.astype(BF16)
    table_lo = jnp.concatenate([last_lo, fill], axis=0).T.astype(BF16)
    onehot_hi = (flat // LANES == subs_of((LANES, total))).astype(F32).astype(BF16)
    found = mm(table_hi, onehot_hi) * 64.0 + mm(table_lo, onehot_hi)
    kept = jnp.where(flat % LANES == subs_of((LANES, total)), found, 0.0)
    picked_last = jnp.sum(kept, axis=0, keepdims=True).astype(jnp.int32)
    for b in range(n // rep):
        last_send[b] = picked_last[:, b * LANES : (b + 1) * LANES]

    @pl.loop(1, n)
    def _(step):
        peer = (me + step) % n
        send(2, last_send.at[peer // rep], last_recv.at[me], peer).start()

    pl.loop(1, half)(functools.partial(serve, 1))
    pl.loop(half, groups)(functools.partial(serve, 6))
    last_recv[pl.ds(me, 1)] = last_send[pl.ds(me // rep, 1)]
    row_recv[pl.ds(me, 1)] = row_send[pl.ds(me, 1)]

    edge_part = mm(edge_ref[...], win_ref[2 * width + time_width :, :]) + bmsg_ref[...]
    chunk = 512

    @pl.loop(0, rows_count // chunk)
    def _(step):
        base = pl.multiple_of(step * chunk, chunk)
        state_ref[pl.ds(base, chunk), :] = mm(mem_ref[pl.ds(base, chunk), :], ghid_ref[...])


    slot_both = jnp.concatenate(slot_row, axis=1)

    @pl.loop(0, groups)
    def _(g):
        placed = slot_both == subs_of((256, 2 * events)) + g * 256
        place_ref[g] = placed.astype(F32).astype(BF16)

    drain(recv_sems.at[2], last_recv)
    got = jnp.concatenate(
        [last_recv[j] for j in range(n)]
        + ([jnp.zeros((LANES - n, LANES), jnp.int32)] if n < LANES else []),
        axis=0,
    )
    got_hi = (got // 64).astype(F32).astype(BF16)
    got_lo = (got % 64).astype(F32).astype(BF16)
    moment = cols[:, 4:5]
    coded = []
    for side in range(2):
        spread = mm(hit_col[side], got_hi) * 64.0 + mm(hit_col[side], got_lo)
        here = pos_col[side] + (me % rep) * slots == lane_e
        before = jnp.sum(jnp.where(here, spread, 0.0), axis=1, keepdims=True)
        angle = (moment - before) * freq_ref[...] + phase_ref[...]
        coded.append(jnp.cos(angle).astype(BF16))

    def settle(sem, buf, blocks_moved):
        part = buf.at[pl.ds(0, blocks_moved)]
        pltpu.make_async_copy(part, part, sem).wait()

    def chosen(steps):
        acc = jnp.zeros((2 * events, width), F32)
        for step in steps:
            g = mirrored(step)
            block = row_recv[pl.ds(g * group, group)].reshape(256, width)
            acc += mm(pick_ref[g], block)
        return acc

    settle(recv_sems.at[6], row_recv, half * group - 1)
    pick_sum[...] = chosen(range(half, groups))
    settle(recv_sems.at[1], row_recv, half * group)
    both = (pick_sum[...] + chosen(range(half))).astype(BF16)
    picked = [both[:events], both[events:]]
    for side in range(2):
        inputs = jnp.concatenate([picked[side], picked[1 - side], coded[side]], axis=1)
        hid = mm(inputs, win_ref[: 2 * width + time_width, :]) + edge_part
        hid = jnp.maximum(hid, 0.0).astype(BF16)
        msgs[side * events : (side + 1) * events, :] = mm(hid, wout_ref[...]).astype(BF16)


    def push(first, stop, kind):
        @pl.loop(first, stop)
        def _(step):
            g = mirrored(step)
            block = mm(place_ref[g], msgs[...])
            msg_send[pl.ds(g * group, group)] = block.astype(BF16).reshape(
                group, slots, block.shape[1]
            )
            for t in range(group):
                peer = g * group + (me + t) % group

                @pl.when(peer != me)
                def _():
                    send(kind, msg_send.at[peer], msg_recv.at[me], peer).start()

    push(0, quarter, 3)
    push(quarter, half, 4)
    push(half, groups, 5)
    msg_recv[pl.ds(me, 1)] = msg_send[pl.ds(me, 1)]
    drain(send_sems.at[0], req_send)
    settle(send_sems.at[1], row_send, half * group)
    settle(send_sems.at[6], row_send, half * group - 1)
    drain(send_sems.at[2], last_recv)

    def gathered(base, steps):
        acc = jnp.zeros((chunk, msgs.shape[1]), F32)
        for step in steps:
            g = mirrored(step)
            block = msg_recv[pl.ds(g * group, group)].reshape(256, msgs.shape[1])
            acc += mm(hits_ref[g, pl.ds(base, chunk), :], block)
        return acc

    @pl.loop(0, rows_count // chunk)
    def _(step):
        base = pl.multiple_of(step * chunk, chunk)
        tally = jnp.zeros((chunk, 256), F32)
        for g in range(groups):
            hits = (flat_ref[g] == subs_of((chunk, 256)) + base).astype(F32)
            hits_ref[g, pl.ds(base, chunk), :] = hits.astype(BF16)
            tally += hits
        count = jnp.sum(tally, axis=1, keepdims=True)
        scale_ref[pl.ds(base, chunk), :] = jnp.where(count > 0.5, 1.0 / jnp.maximum(count, 1.0), -1.0)

    settle(recv_sems.at[5], msg_recv, half * group - 1)

    @pl.loop(0, rows_count // chunk)
    def _(step):
        base = pl.multiple_of(step * chunk, chunk)
        sum_ref[pl.ds(base, chunk), :] = gathered(base, range(half, groups))

    settle(recv_sems.at[3], msg_recv, quarter * group)

    @pl.loop(0, rows_count // chunk)
    def _(step):
        base = pl.multiple_of(step * chunk, chunk)
        sum_ref[pl.ds(base, chunk), :] += gathered(base, range(quarter))

    settle(recv_sems.at[4], msg_recv, (half - quarter) * group)

    @pl.loop(0, rows_count // chunk)
    def _(step):
        base = pl.multiple_of(step * chunk, chunk)
        rows = pl.ds(base, chunk)
        scale = scale_ref[rows, :]
        summed = sum_ref[rows, :] + gathered(base, range(quarter, half))
        mean = (summed * scale).astype(BF16)
        state = mem_ref[rows, :].astype(F32)
        gi = mm(mean, gin_ref[...]) + bgru_ref[...].reshape(1, 3 * width)
        gh = state_ref[rows, :]
        reset = 0.5 * jnp.tanh(0.5 * (gi[:, :width] + gh[:, :width])) + 0.5
        update = 0.5 * jnp.tanh(0.5 * (gi[:, width : 2 * width] + gh[:, width : 2 * width])) + 0.5
        candid = jnp.tanh(gi[:, 2 * width :] + reset * gh[:, 2 * width :])
        fresh = candid + update * (state - candid)
        out_ref[rows, :] = jnp.where(scale > 0.0, fresh, state).astype(BF16)
        pltpu.make_async_copy(out_ref.at[rows], out_hbm.at[rows], store_sem).start()

    settle(send_sems.at[3], msg_send, quarter * group)
    settle(send_sems.at[4], msg_send, (half - quarter) * group)
    settle(send_sems.at[5], msg_send, half * group - 1)
    pltpu.make_async_copy(out_ref, out_hbm, store_sem).wait()


def local(
    per_row,
    src_owner,
    src_row,
    dst_owner,
    dst_row,
    event_time,
    edge_feat,
    memory,
    last_update,
    time_freq,
    time_phase,
    w_msg_in,
    b_msg,
    w_msg_out,
    w_gru_in,
    b_gru_in,
    w_gru_hid,
):
    n = lax.axis_size(("ev", "node"))
    events = edge_feat.shape[0]
    slots = 2 * max(2, 2 * events // n)
    rows_count, width = memory.shape
    msg_width = w_msg_out.shape[1]
    total = n * slots
    operands = (
        src_owner.reshape(1, events),
        dst_owner.reshape(1, events),
        src_row.reshape(1, events),
        dst_row.reshape(1, events),
        event_time.reshape(1, events),
        time_freq.reshape(1, -1),
        time_phase.reshape(1, -1),
        b_msg.reshape(1, -1),
        b_gru_in,
        last_update.reshape(rows_count // LANES, LANES),
        memory,
        edge_feat,
        w_msg_in,
        w_msg_out,
        w_gru_in,
        w_gru_hid,
    )
    anywhere = pl.BlockSpec(memory_space=pl.ANY)
    return pl.pallas_call(
        functools.partial(exchange_kernel, n, per_row, slots, events, time_freq.shape[0]),
        out_shape=jax.ShapeDtypeStruct(memory.shape, BF16),
        in_specs=[anywhere] * len(operands),
        out_specs=anywhere,
        scratch_shapes=[pltpu.VMEM(x.shape, x.dtype) for x in operands]
        + [
            pltpu.VMEM(memory.shape, BF16),
            pltpu.VMEM((n, 1, LANES), jnp.int32),
            pltpu.VMEM((n, 1, LANES), jnp.int32),
            pltpu.VMEM((total, 1), jnp.int32),
            pltpu.VMEM((total // 256, 2 * events, 256), BF16),
            pltpu.VMEM((total // 256, 256, 2 * events), BF16),
            pltpu.VMEM((2 * events, width), F32),
            pltpu.VMEM((n * slots // LANES, 1, LANES), jnp.int32),
            pltpu.VMEM((n, 1, LANES), jnp.int32),
            pltpu.VMEM((n, slots, width), BF16),
            pltpu.VMEM((n, slots, width), BF16),
            pltpu.VMEM((n, slots, msg_width), BF16),
            pltpu.VMEM((n, slots, msg_width), BF16),
            pltpu.VMEM((2 * events, msg_width), BF16),
            pltpu.VMEM((total // 256, 1, 256), jnp.int32),
            pltpu.VMEM((total // 256, rows_count, 256), BF16),
            pltpu.VMEM((rows_count, 1), F32),
            pltpu.VMEM((rows_count, 3 * width), F32),
            pltpu.VMEM((rows_count, msg_width), F32),
            pltpu.SemaphoreType.DMA((7,)),
            pltpu.SemaphoreType.DMA((7,)),
            pltpu.SemaphoreType.DMA((len(operands),)),
            pltpu.SemaphoreType.DMA,
        ],
        compiler_params=pltpu.CompilerParams(
            collective_id=0, has_side_effects=True, vmem_limit_bytes=60 * 1024 * 1024
        ),
        name="exchange",
    )(*operands)


def solution(mesh):
    in_specs = (
        P(("ev", "node"), None),
        P(("ev", "node")),
        P(("ev", "node"), None),
        P(("ev", "node")),
        P(("ev", "node")),
        P(("ev", "node"), None),
        P(("ev", "node"), None),
        P(("ev", "node")),
        P(),
        P(),
        P(),
        P(),
        P(),
        P(),
        P(),
        P(),
    )
    out_specs = P(("ev", "node"), None)
    return jax.shard_map(
        functools.partial(local, mesh.shape["node"]),
        mesh=mesh,
        in_specs=in_specs,
        out_specs=out_specs,
        check_vma=False,
    )
```

```python
import functools

import jax
import jax.numpy as jnp
from jax import lax
from jax.experimental import pallas as pl
from jax.experimental.pallas import tpu as pltpu
from jax.sharding import PartitionSpec as P

MESH = pl.DeviceIdType.MESH
LANES = 128
F32 = jnp.float32
BF16 = jnp.bfloat16


def mm(a, b):
    return jnp.dot(a, b, preferred_element_type=F32)


def lanes_of(shape):
    return lax.broadcasted_iota(jnp.int32, shape, 1)


def subs_of(shape):
    return lax.broadcasted_iota(jnp.int32, shape, 0)


def exchange_kernel(
    n,
    per_row,
    slots,
    events,
    time_width,
    so_hbm,
    do_hbm,
    sr_hbm,
    dr_hbm,
    et_hbm,
    freq_hbm,
    phase_hbm,
    bmsg_hbm,
    bgru_hbm,
    last_hbm,
    mem_hbm,
    edge_hbm,
    win_hbm,
    wout_hbm,
    gin_hbm,
    ghid_hbm,
    out_hbm,
    so_ref,
    do_ref,
    sr_ref,
    dr_ref,
    et_ref,
    freq_ref,
    phase_ref,
    bmsg_ref,
    bgru_ref,
    last_ref,
    mem_ref,
    edge_ref,
    win_ref,
    wout_ref,
    gin_ref,
    ghid_ref,
    out_ref,
    req_send,
    req_recv,
    rows_col,
    pick_ref,
    place_ref,
    pick_sum,
    last_send,
    last_recv,
    row_send,
    row_recv,
    msg_send,
    msg_recv,
    msgs,
    flat_ref,
    hits_ref,
    scale_ref,
    state_ref,
    sum_ref,
    send_sems,
    recv_sems,
    load_sems,
    store_sem,
):
    ev = lax.axis_index("ev")
    me = ev * per_row + lax.axis_index("node")
    rows_count, width = mem_ref.shape
    hidden = wout_ref.shape[0]
    cap = slots // 2
    rep = LANES // slots
    total = n * slots
    group = 256 // slots
    groups = n // group

    def coords(device):
        return (device // per_row, device % per_row)

    half = groups // 2
    quarter = half - 1

    def mirrored(step):
        far, near = half + (step + half // 2) % half, groups - 1 - step
        k = far + (step // half) * (near - far)
        g, unit = 0, 1
        while unit < groups:
            g = g + unit * ((me // group // unit + k // unit) % 2)
            unit = 2 * unit
        return g

    barrier = pltpu.get_barrier_semaphore()

    loads = [
        pltpu.make_async_copy(src, dst, load_sems.at[k])
        for k, (src, dst) in enumerate(
            [
                (so_hbm, so_ref),
                (do_hbm, do_ref),
                (sr_hbm, sr_ref),
                (dr_hbm, dr_ref),
                (et_hbm, et_ref),
                (last_hbm, last_ref),
                (freq_hbm, freq_ref),
                (phase_hbm, phase_ref),
                (bmsg_hbm, bmsg_ref),
                (bgru_hbm, bgru_ref),
                (mem_hbm, mem_ref),
                (edge_hbm, edge_ref),
                (win_hbm, win_ref),
                (wout_hbm, wout_ref),
                (ghid_hbm, ghid_ref),
                (gin_hbm, gin_ref),
            ]
        )
    ]
    for load in loads:
        load.start()
    @pl.loop(1, n)
    def _(step):
        pl.semaphore_signal(
            barrier, inc=1, device_id=coords((me + step) % n), device_id_type=MESH
        )

    for load in loads[:5]:
        load.wait()
    ints = jnp.concatenate(
        [so_ref[...], do_ref[...], sr_ref[...], dr_ref[...], et_ref[...]]
        + [jnp.zeros((3, events), jnp.int32)],
        axis=0,
    )
    padded = jnp.concatenate(
        [ints.astype(F32), jnp.zeros((LANES - 8, events), F32)], axis=0
    )
    cols = padded.T
    lane_e = lanes_of((events, LANES))
    sub_e = subs_of((LANES, events))
    tri_low = (lanes_of((events, events)) < subs_of((events, events))).astype(F32).astype(BF16)
    tri_up = (subs_of((events, events)) < lanes_of((events, events))).astype(F32).astype(BF16)

    hit_col, pos_col, slot_col, slot_row = [], [], [], []
    req_hi = jnp.zeros((LANES, LANES), F32)
    req_lo = jnp.zeros((LANES, LANES), F32)
    for side in range(2):
        owner_c = cols[:, side : side + 1].astype(jnp.int32)
        row_c = cols[:, 2 + side : 3 + side].astype(jnp.int32)
        hit_c = (owner_c == lane_e).astype(F32)
        hit_cb = hit_c.astype(BF16)
        pos_c = jnp.sum(mm(tri_low, hit_cb) * hit_c, axis=1, keepdims=True).astype(jnp.int32)
        pos_c = pos_c + side * cap
        owner_r = ints[side : side + 1, :]
        hit_r = (owner_r == sub_e).astype(F32)
        hit_rb = hit_r.astype(BF16)
        pos_r = jnp.sum(mm(hit_rb, tri_up) * hit_r, axis=0, keepdims=True).astype(jnp.int32)
        pos_r = pos_r + side * cap
        place = pos_c == lane_e % slots
        req_hi += mm(hit_rb, jnp.where(place, (row_c // 64 + 1).astype(F32), 0.0).astype(BF16))
        req_lo += mm(hit_rb, jnp.where(place, (row_c % 64).astype(F32), 0.0).astype(BF16))
        hit_col.append(hit_cb)
        pos_col.append(pos_c)
        slot_col.append(owner_c * slots + pos_c)
        slot_row.append(owner_r * slots + pos_r)
    request = jnp.where(req_hi > 0.5, (req_hi - 1.0) * 64.0 + req_lo, -1.0).astype(jnp.int32)
    for j in range(n):
        req_send[j] = request[j : j + 1, :]

    pl.semaphore_wait(barrier, n - 1)

    def send(phase, src, dst, device):
        return pltpu.make_async_remote_copy(
            src_ref=src,
            dst_ref=dst,
            send_sem=send_sems.at[phase],
            recv_sem=recv_sems.at[phase],
            device_id=coords(device),
            device_id_type=MESH,
        )

    def drain(sem, buf):
        part = buf.at[pl.ds(0, n - 1)]
        pltpu.make_async_copy(part, part, sem).wait()

    @pl.loop(1, n)
    def _(step):
        peer = (me + step) % n
        send(0, req_send.at[peer], req_recv.at[me], peer).start()

    for side in range(2):
        for g in range(groups):
            near = slot_col[side] == lanes_of((events, 256)) + g * 256
            pick_ref[g, side * events : (side + 1) * events, :] = near.astype(F32).astype(BF16)

    req_recv[pl.ds(me, 1)] = req_send[pl.ds(me, 1)]
    drain(recv_sems.at[0], req_recv)

    lane_1 = lanes_of((1, LANES))
    blocks = []
    for b in range(n // rep):
        block = req_recv[b * rep]
        for q in range(1, rep):
            block = jnp.where(lane_1 // slots == q, req_recv[b * rep + q], block)
        blocks.append(block)
    flat = jnp.concatenate(blocks, axis=1)
    for g in range(groups):
        flat_ref[g] = flat[:, g * 256 : (g + 1) * 256]
    square = jnp.concatenate(
        [req_recv[j].astype(F32) for j in range(n)]
        + ([jnp.zeros((LANES - n, LANES), F32)] if n < LANES else []),
        axis=0,
    ).T.astype(jnp.int32)
    for j in range(n):
        rows_col[j * slots : (j + 1) * slots, :] = square[:slots, j : j + 1]

    for load in loads[5:]:
        load.wait()

    def serve(kind, step):
        g = mirrored(step)
        wanted = rows_col[pl.ds(pl.multiple_of(g * 256, 256), 256), :]
        acc = jnp.zeros((256, width), F32)
        depth = 1024
        for k in range(rows_count // depth):
            onehot = (wanted == lanes_of((256, depth)) + k * depth).astype(F32).astype(BF16)
            acc += mm(onehot, mem_ref[k * depth : (k + 1) * depth, :])
        row_send[pl.ds(g * group, group)] = acc.astype(BF16).reshape(group, slots, width)
        for t in range(group):
            peer = g * group + (me + t) % group

            @pl.when(peer != me)
            def _():
                send(kind, row_send.at[peer], row_recv.at[me], peer).start()

    serve(1, 0)
    last = last_ref[...]
    high_count = rows_count // LANES
    last_hi = (last // 64).astype(F32)
    last_lo = (last % 64).astype(F32)
    fill = jnp.zeros((LANES - high_count, LANES), F32)
    table_hi = jnp.concatenate([last_hi, fill], axis=0).T.astype(BF16)
    table_lo = jnp.concatenate([last_lo, fill], axis=0).T.astype(BF16)
    onehot_hi = (flat // LANES == subs_of((LANES, total))).astype(F32).astype(BF16)
    found = mm(table_hi, onehot_hi) * 64.0 + mm(table_lo, onehot_hi)
    kept = jnp.where(flat % LANES == subs_of((LANES, total)), found, 0.0)
    picked_last = jnp.sum(kept, axis=0, keepdims=True).astype(jnp.int32)
    for b in range(n // rep):
        last_send[b] = picked_last[:, b * LANES : (b + 1) * LANES]

    @pl.loop(1, n)
    def _(step):
        peer = (me + step) % n
        send(2, last_send.at[peer // rep], last_recv.at[me], peer).start()

    pl.loop(1, half)(functools.partial(serve, 1))
    pl.loop(half, groups)(functools.partial(serve, 6))
    last_recv[pl.ds(me, 1)] = last_send[pl.ds(me // rep, 1)]
    row_recv[pl.ds(me, 1)] = row_send[pl.ds(me, 1)]

    edge_part = mm(edge_ref[...], win_ref[2 * width + time_width :, :]) + bmsg_ref[...]
    chunk = 512

    @pl.loop(0, rows_count // chunk)
    def _(step):
        base = pl.multiple_of(step * chunk, chunk)
        state_ref[pl.ds(base, chunk), :] = mm(mem_ref[pl.ds(base, chunk), :], ghid_ref[...])


    slot_both = jnp.concatenate(slot_row, axis=1)

    @pl.loop(0, groups)
    def _(g):
        placed = slot_both == subs_of((256, 2 * events)) + g * 256
        place_ref[g] = placed.astype(F32).astype(BF16)

    drain(recv_sems.at[2], last_recv)
    got = jnp.concatenate(
        [last_recv[j] for j in range(n)]
        + ([jnp.zeros((LANES - n, LANES), jnp.int32)] if n < LANES else []),
        axis=0,
    )
    got_hi = (got // 64).astype(F32).astype(BF16)
    got_lo = (got % 64).astype(F32).astype(BF16)
    moment = cols[:, 4:5]
    coded = []
    for side in range(2):
        spread = mm(hit_col[side], got_hi) * 64.0 + mm(hit_col[side], got_lo)
        here = pos_col[side] + (me % rep) * slots == lane_e
        before = jnp.sum(jnp.where(here, spread, 0.0), axis=1, keepdims=True)
        angle = (moment - before) * freq_ref[...] + phase_ref[...]
        coded.append(jnp.cos(angle).astype(BF16))

    def settle(sem, buf, blocks_moved):
        part = buf.at[pl.ds(0, blocks_moved)]
        pltpu.make_async_copy(part, part, sem).wait()

    def chosen(steps):
        acc = jnp.zeros((2 * events, width), F32)
        for step in steps:
            g = mirrored(step)
            block = row_recv[pl.ds(g * group, group)].reshape(256, width)
            acc += mm(pick_ref[g], block)
        return acc

    settle(recv_sems.at[6], row_recv, half * group - 1)
    pick_sum[...] = chosen(range(half, groups))
    settle(recv_sems.at[1], row_recv, half * group)
    both = (pick_sum[...] + chosen(range(half))).astype(BF16)
    picked = [both[:events], both[events:]]
    for side in range(2):
        inputs = jnp.concatenate([picked[side], picked[1 - side], coded[side]], axis=1)
        hid = mm(inputs, win_ref[: 2 * width + time_width, :]) + edge_part
        hid = jnp.maximum(hid, 0.0).astype(BF16)
        msgs[side * events : (side + 1) * events, :] = mm(hid, wout_ref[...]).astype(BF16)


    def push(first, stop, kind):
        @pl.loop(first, stop)
        def _(step):
            g = mirrored(step)
            block = mm(place_ref[g], msgs[...])
            msg_send[pl.ds(g * group, group)] = block.astype(BF16).reshape(
                group, slots, block.shape[1]
            )
            for t in range(group):
                peer = g * group + (me + t) % group

                @pl.when(peer != me)
                def _():
                    send(kind, msg_send.at[peer], msg_recv.at[me], peer).start()

    push(0, quarter, 3)
    push(quarter, half, 4)
    push(half, groups, 5)
    msg_recv[pl.ds(me, 1)] = msg_send[pl.ds(me, 1)]
    drain(send_sems.at[0], req_send)
    settle(send_sems.at[1], row_send, half * group)
    settle(send_sems.at[6], row_send, half * group - 1)
    drain(send_sems.at[2], last_recv)

    def gathered(base, steps):
        acc = jnp.zeros((chunk, msgs.shape[1]), F32)
        for step in steps:
            g = mirrored(step)
            block = msg_recv[pl.ds(g * group, group)].reshape(256, msgs.shape[1])
            acc += mm(hits_ref[g, pl.ds(base, chunk), :], block)
        return acc

    @pl.loop(0, rows_count // chunk)
    def _(step):
        base = pl.multiple_of(step * chunk, chunk)
        tally = jnp.zeros((chunk, 256), F32)
        for g in range(groups):
            hits = (flat_ref[g] == subs_of((chunk, 256)) + base).astype(F32)
            hits_ref[g, pl.ds(base, chunk), :] = hits.astype(BF16)
            tally += hits
        count = jnp.sum(tally, axis=1, keepdims=True)
        scale_ref[pl.ds(base, chunk), :] = jnp.where(count > 0.5, 1.0 / jnp.maximum(count, 1.0), -1.0)

    settle(recv_sems.at[5], msg_recv, half * group - 1)

    @pl.loop(0, rows_count // chunk)
    def _(step):
        base = pl.multiple_of(step * chunk, chunk)
        sum_ref[pl.ds(base, chunk), :] = gathered(base, range(half, groups))

    settle(recv_sems.at[3], msg_recv, quarter * group)

    @pl.loop(0, rows_count // chunk)
    def _(step):
        base = pl.multiple_of(step * chunk, chunk)
        sum_ref[pl.ds(base, chunk), :] += gathered(base, range(quarter))

    settle(recv_sems.at[4], msg_recv, (half - quarter) * group)

    @pl.loop(0, rows_count // chunk)
    def _(step):
        base = pl.multiple_of(step * chunk, chunk)
        rows = pl.ds(base, chunk)
        scale = scale_ref[rows, :]
        summed = sum_ref[rows, :] + gathered(base, range(quarter, half))
        mean = (summed * scale).astype(BF16)
        state = mem_ref[rows, :].astype(F32)
        gi = mm(mean, gin_ref[...]) + bgru_ref[...].reshape(1, 3 * width)
        gh = state_ref[rows, :]
        reset = 0.5 * jnp.tanh(0.5 * (gi[:, :width] + gh[:, :width])) + 0.5
        update = 0.5 * jnp.tanh(0.5 * (gi[:, width : 2 * width] + gh[:, width : 2 * width])) + 0.5
        candid = jnp.tanh(gi[:, 2 * width :] + reset * gh[:, 2 * width :])
        fresh = candid + update * (state - candid)
        out_ref[rows, :] = jnp.where(scale > 0.0, fresh, state).astype(BF16)
        pltpu.make_async_copy(out_ref.at[rows], out_hbm.at[rows], store_sem).start()

    settle(send_sems.at[3], msg_send, quarter * group)
    settle(send_sems.at[4], msg_send, (half - quarter) * group)
    settle(send_sems.at[5], msg_send, half * group - 1)
    pltpu.make_async_copy(out_ref, out_hbm, store_sem).wait()


def local(
    per_row,
    src_owner,
    src_row,
    dst_owner,
    dst_row,
    event_time,
    edge_feat,
    memory,
    last_update,
    time_freq,
    time_phase,
    w_msg_in,
    b_msg,
    w_msg_out,
    w_gru_in,
    b_gru_in,
    w_gru_hid,
):
    n = lax.axis_size(("ev", "node"))
    events = edge_feat.shape[0]
    slots = 2 * max(2, 2 * events // n)
    rows_count, width = memory.shape
    msg_width = w_msg_out.shape[1]
    total = n * slots
    operands = (
        src_owner.reshape(1, events),
        dst_owner.reshape(1, events),
        src_row.reshape(1, events),
        dst_row.reshape(1, events),
        event_time.reshape(1, events),
        time_freq.reshape(1, -1),
        time_phase.reshape(1, -1),
        b_msg.reshape(1, -1),
        b_gru_in,
        last_update.reshape(rows_count // LANES, LANES),
        memory,
        edge_feat,
        w_msg_in,
        w_msg_out,
        w_gru_in,
        w_gru_hid,
    )
    anywhere = pl.BlockSpec(memory_space=pl.ANY)
    return pl.pallas_call(
        functools.partial(exchange_kernel, n, per_row, slots, events, time_freq.shape[0]),
        out_shape=jax.ShapeDtypeStruct(memory.shape, BF16),
        in_specs=[anywhere] * len(operands),
        out_specs=anywhere,
        scratch_shapes=[pltpu.VMEM(x.shape, x.dtype) for x in operands]
        + [
            pltpu.VMEM(memory.shape, BF16),
            pltpu.VMEM((n, 1, LANES), jnp.int32),
            pltpu.VMEM((n, 1, LANES), jnp.int32),
            pltpu.VMEM((total, 1), jnp.int32),
            pltpu.VMEM((total // 256, 2 * events, 256), BF16),
            pltpu.VMEM((total // 256, 256, 2 * events), BF16),
            pltpu.VMEM((2 * events, width), F32),
            pltpu.VMEM((n * slots // LANES, 1, LANES), jnp.int32),
            pltpu.VMEM((n, 1, LANES), jnp.int32),
            pltpu.VMEM((n, slots, width), BF16),
            pltpu.VMEM((n, slots, width), BF16),
            pltpu.VMEM((n, slots, msg_width), BF16),
            pltpu.VMEM((n, slots, msg_width), BF16),
            pltpu.VMEM((2 * events, msg_width), BF16),
            pltpu.VMEM((total // 256, 1, 256), jnp.int32),
            pltpu.VMEM((total // 256, rows_count, 256), BF16),
            pltpu.VMEM((rows_count, 1), F32),
            pltpu.VMEM((rows_count, 3 * width), F32),
            pltpu.VMEM((rows_count, msg_width), F32),
            pltpu.SemaphoreType.DMA((7,)),
            pltpu.SemaphoreType.DMA((7,)),
            pltpu.SemaphoreType.DMA((len(operands),)),
            pltpu.SemaphoreType.DMA,
        ],
        compiler_params=pltpu.CompilerParams(
            collective_id=0, has_side_effects=True, vmem_limit_bytes=60 * 1024 * 1024
        ),
        name="exchange",
    )(*operands)


def solution(mesh):
    in_specs = (
        P(("ev", "node"), None),
        P(("ev", "node")),
        P(("ev", "node"), None),
        P(("ev", "node")),
        P(("ev", "node")),
        P(("ev", "node"), None),
        P(("ev", "node"), None),
        P(("ev", "node")),
        P(),
        P(),
        P(),
        P(),
        P(),
        P(),
        P(),
        P(),
    )
    out_specs = P(("ev", "node"), None)
    return jax.shard_map(
        functools.partial(local, mesh.shape["node"]),
        mesh=mesh,
        in_specs=in_specs,
        out_specs=out_specs,
        check_vma=False,
    )
```
